32 devices in a mesh: req: 16 (over z, x, core), tp: 2 (over y).
Axes of the slice: x: 2, y: 2, z: 4, core: 2. Of those that a mesh axis runs over, the one named last changes fastest.
Arguments:
- query: bfloat16 [1792, 3072], P('req', 'tp'), may hold values from -48 to 48
- key: bfloat16 [1792, 3072], P('req', 'tp'), may hold values from -12 to 12
- value: bfloat16 [1792, 3072], P('req', 'tp'), may hold values from -6 to 6
- cross_query: bfloat16 [1792, 3072], P('req', 'tp'), may hold values from -48 to 48
- text_key: bfloat16 [2048, 3072], P('req', 'tp'), may hold values from -12 to 12
- text_value: bfloat16 [2048, 3072], P('req', 'tp'), may hold values from -6 to 6
- wo_self: bfloat16 [3072, 5120], P('tp', 'req'), may hold values from -3 to 3
- wo_cross: bfloat16 [3072, 5120], P('tp', 'req'), may hold values from -3 to 3
- attn_gate: float32 [4, 5120], replicated, may hold values from 0.5 to 1.5
- mix_coef: float32 [5120], P('tp'), may hold values from 0.1 to 0.4
- latent: bfloat16 [1792, 5120], P('req', 'tp'), may hold values from -6 to 6
- tenant_len: int32 [4], replicated, may hold values from 1 to 448, as said below
- text_len: int32 [4], replicated, may hold values from 2 to 512, as said below
- t_index: int32 [4], replicated, may hold values from 0 to 49
Outputs:
- velocity: bfloat16 [1792, 5120], P('req', 'tp')
- updated: float32 [1792, 5120], P('req', 'tp')
The draws below stay inside these ranges and needn't reach their ends.
Inputs may be any that keep to these rules, and one draw needn't show every extreme that they name: `tenant_len`: tenant t's latent tokens fill the slots of req indices t, t + 4, t + 8, ... in order from the first slot; one tenant fills all 448 slots. `text_len`: one tenant's prompt has all 512 tokens.
All inputs are finite; a program needn't handle non-finite values.
Results may differ from the reference program's by a relative error of at most 0.019.
Values may be sent and summed in bfloat16 or wider, within the bound.
A program may use at most 128 MiB of HBM per device.

```python
import math
import jax
import jax.numpy as jnp
from jax import lax

D = 5120
HEADS = 24
DH = 128
TEXT = 512
TENANTS = 4
STEPS = 50
TILE = 112
GROUP = 4
TOKENS = 1792
N_REQ = 16
N_TP = 2


def latent_pair(key):
    width = HEADS * DH
    keys = jax.random.truncated_normal(jax.random.fold_in(key, 11), -6.0, 6.0, (TOKENS, width), jnp.float32)
    queries = jax.random.truncated_normal(jax.random.fold_in(key, 12), -6.0, 6.0, (TOKENS, width), jnp.float32)
    return (queries, keys)


def text_pair(key):
    width = HEADS * DH
    rows_all = TENANTS * TEXT
    tkeys = jax.random.truncated_normal(jax.random.fold_in(key, 21), -6.0, 6.0, (rows_all, width), jnp.float32)
    queries = jax.random.truncated_normal(jax.random.fold_in(key, 22), -6.0, 6.0, (TOKENS, width), jnp.float32)
    return (queries, tkeys)


def draw_query(key, part):
    return latent_pair(key)[0].astype(jnp.bfloat16)


def draw_key(key, part):
    return latent_pair(key)[1].astype(jnp.bfloat16)


def draw_cross_query(key, part):
    return text_pair(key)[0].astype(jnp.bfloat16)


def draw_text_key(key, part):
    return text_pair(key)[1].astype(jnp.bfloat16)


def draw_tenant_len(key, part):
    full = GROUP * TILE
    quarter = full // TENANTS
    order = jax.random.permutation(jax.random.fold_in(key, 31), TENANTS)
    jitter = jax.random.randint(jax.random.fold_in(key, 32), (TENANTS,), 0, TILE // 2 + 1)
    small = jax.random.randint(jax.random.fold_in(key, 33), (TENANTS,), 1, quarter + 1)
    base = full * (TENANTS - order) // TENANTS - jitter
    base = jnp.where(order == TENANTS - 1, small, base)
    return jnp.where(order == 0, full, jnp.maximum(base, 1)).astype(jnp.int32)


def draw_text_len(key, part):
    lens = jax.random.randint(jax.random.fold_in(key, 41), (TENANTS,), 2, TEXT + 1)
    which = jax.random.randint(jax.random.fold_in(key, 42), (), 0, TENANTS)
    return jnp.where(jnp.arange(TENANTS) == which, TEXT, lens).astype(jnp.int32)


def plant(values, rng, least, high):
    index_at = [jax.random.randint(jax.random.fold_in(rng, axis), (), 0, length) for axis, length in enumerate(values.shape)]
    main_axis = values.shape.index(max(values.shape))
    next_to = index_at[:main_axis] + [(index_at[main_axis] + 1) % values.shape[main_axis]] + index_at[main_axis + 1:]
    return values.at[tuple(index_at)].set(least).at[tuple(next_to)].set(high)


def levels(key, dims, shards, low, top_value):
    loudness, own = 1.0, jax.random.fold_in(key, 6)
    for position, shards_of in shards:
        heights = jnp.exp(jax.random.uniform(jax.random.fold_in(own, position), (shards_of,), jnp.float32, low / len(shards), top_value / len(shards)))
        loudness = loudness * jnp.repeat(heights, dims[position] // shards_of).reshape([-1 if axis == position else 1 for axis in range(len(dims))])
    return loudness


def noise(rng, dims, spread, reach, shards=(), kind=jnp.bfloat16):
    loudness = levels(rng, dims, shards, -0.22, 0.18) if shards else 1.0
    entries = jax.random.normal(rng, dims, jnp.float32) * spread * loudness
    return jnp.minimum(jnp.maximum(entries, -reach), reach).astype(kind)


def setup_inputs(seed: int = 0) -> dict:
    splits = jax.random.split(jax.random.key(seed), 15)
    return {
        "query": draw_query(jax.random.fold_in(splits[14], 71), 0),
        "key": draw_key(jax.random.fold_in(splits[14], 71), 0),
        "value": noise(splits[2], (TOKENS, HEADS * DH), 1.0, 6.0, ((0, 16), (1, 2))),
        "cross_query": draw_cross_query(jax.random.fold_in(splits[14], 71), 0),
        "text_key": draw_text_key(jax.random.fold_in(splits[14], 71), 0),
        "text_value": noise(splits[5], (TENANTS * TEXT, HEADS * DH), 1.0, 6.0, ((0, 16), (1, 2))),
        "wo_self": noise(splits[6], (HEADS * DH, D), 0.5, 3.0, ((0, 2), (1, 16))),
        "wo_cross": noise(splits[7], (HEADS * DH, D), 0.5, 3.0, ((0, 2), (1, 16))),
        "attn_gate": jnp.clip(jax.random.uniform(splits[8], (TENANTS, D), jnp.float32, 0.5, 1.5), 0.5, 1.5),
        "mix_coef": jnp.clip(jnp.exp(math.log(0.4) - 1.3862944 * jax.random.uniform(splits[9], (D,), jnp.float32) ** levels(splits[9], (D,), ((0, 2),), -0.2, 0.2)), 0.1, 0.4),
        "latent": noise(splits[10], (TOKENS, D), 1.0, 6.0, ((0, 16), (1, 2))),
        "tenant_len": draw_tenant_len(jax.random.fold_in(splits[14], 71), 0),
        "text_len": draw_text_len(jax.random.fold_in(splits[14], 71), 0),
        "t_index": plant(jax.random.randint(splits[13], (TENANTS,), 0, STEPS), jax.random.fold_in(splits[13], 1), 0, STEPS - 1).astype(jnp.int32),
    }


def attend(queries, keys, values, valid):
    heads = queries.shape[1] // DH
    q_heads = queries.reshape(queries.shape[0], heads, DH).transpose(1, 0, 2)
    k_heads = keys.reshape(keys.shape[0], heads, DH).transpose(1, 0, 2)
    v_heads = values.reshape(values.shape[0], heads, DH).transpose(1, 0, 2)
    scale = 1.0 / (DH ** 0.5)

    def one_head(items):
        q_one, k_one, v_one = items
        scores = jnp.dot(q_one, k_one.T, preferred_element_type=jnp.float32) * scale
        scores = jnp.where(valid[None, :], scores, -1e30)
        top = jnp.max(scores, axis=-1, keepdims=True)
        weights = jnp.where(valid[None, :], jnp.exp(scores - top), 0.0)
        denom = jnp.sum(weights, axis=-1, keepdims=True)
        mixed = jnp.dot(weights.astype(jnp.bfloat16), v_one, preferred_element_type=jnp.float32)
        return (mixed / denom).astype(jnp.bfloat16)

    out = lax.map(one_head, (q_heads, k_heads, v_heads))
    return out.transpose(1, 0, 2).reshape(queries.shape[0], heads * DH)


def tenant_rows(array, per_dev, tenant):
    group = array.shape[0] // (per_dev * TENANTS)
    return array.reshape(group, TENANTS, per_dev, array.shape[1])[:, tenant].reshape(group * per_dev, array.shape[1])


def reference(query, key, value, cross_query, text_key, text_value, wo_self, wo_cross, attn_gate, mix_coef, latent, tenant_len, text_len, t_index):
    group = N_REQ // TENANTS
    text_dev = TEXT // group
    width = HEADS * DH // N_TP
    vel_list = []
    upd_list = []
    for tenant in range(TENANTS):
        q_t = tenant_rows(query, TILE, tenant)
        k_t = tenant_rows(key, TILE, tenant)
        v_t = tenant_rows(value, TILE, tenant)
        cq_t = tenant_rows(cross_query, TILE, tenant)
        tk_t = tenant_rows(text_key, text_dev, tenant)
        tv_t = tenant_rows(text_value, text_dev, tenant)
        lat_t = tenant_rows(latent, TILE, tenant)
        positions = jnp.arange(group * TILE, dtype=jnp.int32)
        valid = positions < tenant_len[tenant]
        text_valid = jnp.arange(TEXT, dtype=jnp.int32) < text_len[tenant]
        self_out = attend(q_t, k_t, v_t, valid)
        cross_out = attend(cq_t, tk_t, tv_t, text_valid)
        gate = attn_gate[tenant]
        total = jnp.zeros((group * TILE, D), jnp.float32)
        for part in range(N_TP):
            lo = part * width
            s_term = jnp.dot(self_out[:, lo:lo + width], wo_self[lo:lo + width], preferred_element_type=jnp.float32)
            c_term = jnp.dot(cross_out[:, lo:lo + width], wo_cross[lo:lo + width], preferred_element_type=jnp.float32)
            rounded = lax.optimization_barrier((gate[None, :] * s_term + c_term).astype(jnp.bfloat16))
            total = total + rounded.astype(jnp.float32)
        branch = jnp.where(valid[:, None], total.astype(jnp.bfloat16), jnp.zeros((), jnp.bfloat16))
        branch32 = branch.astype(jnp.float32)
        padded = jnp.pad(branch32, ((1, 1), (0, 0)))
        vel = branch32 + mix_coef[None, :] * (padded[:-2] + padded[2:] - 2.0 * branch32)
        vel = jnp.where(valid[:, None], vel, 0.0)
        frac = 1.0 - t_index[tenant].astype(jnp.float32) / STEPS
        sigma = 5.0 * frac / (1.0 + 4.0 * frac)
        upd = lat_t.astype(jnp.float32) + sigma * vel
        vel_list.append(vel.astype(jnp.bfloat16).reshape(group, TILE, D))
        upd_list.append(upd.reshape(group, TILE, D))
    velocity = jnp.stack(vel_list, axis=1).reshape(group * TENANTS * TILE, D)
    updated = jnp.stack(upd_list, axis=1).reshape(group * TENANTS * TILE, D)
    return velocity, updated
```

```python
import functools

import jax
import jax.numpy as jnp
from jax import lax
from jax.experimental import pallas as pl
from jax.experimental.pallas import tpu as pltpu
from jax.sharding import PartitionSpec as P

DH = 128
TENANTS = 4
STEPS = 50


def passed_along(block, axis, distance):
    devices = range(lax.axis_size(axis))
    route = [((i - distance) % len(devices), i) for i in devices]
    return lax.ppermute(block, axis, route)


def shifted(block, axis, distance):
    devices = range(lax.axis_size(axis))
    route = [(i - distance, i) for i in devices if i - distance in devices]
    return lax.ppermute(block, axis, route)


def attend_block(state, q_heads, k_block, v_block, valid):
    top, denom, accum = state
    heads = q_heads.shape[1]
    k_heads = k_block.reshape(k_block.shape[0], heads, DH)
    v_heads = v_block.reshape(v_block.shape[0], heads, DH)
    scores = jnp.einsum("qhd,khd->hqk", q_heads, k_heads, preferred_element_type=jnp.float32) * (
        1.0 / DH**0.5
    )
    scores = jnp.where(valid[None, None, :], scores, -1e30)
    new_top = jnp.maximum(top, jnp.max(scores, axis=-1))
    weights = jnp.where(valid[None, None, :], jnp.exp(scores - new_top[..., None]), 0.0)
    factor = jnp.exp(top - new_top)
    denom = denom * factor + jnp.sum(weights, axis=-1)
    mixed = jnp.einsum(
        "hqk,khd->hqd", weights.astype(jnp.bfloat16), v_heads, preferred_element_type=jnp.float32
    )
    return (new_top, denom, accum * factor[..., None] + mixed)


def finish(state, tiles, feat):
    top, denom, accum = state
    out = accum / denom[..., None]
    return out.transpose(1, 0, 2).reshape(tiles, feat).astype(jnp.bfloat16)


def shards(
    query,
    key,
    value,
    cross_query,
    text_key,
    text_value,
    wo_self,
    wo_cross,
    attn_gate,
    mix_coef,
    latent,
    tenant_len,
    text_len,
    t_index,
):
    tiles, feat = query.shape
    text_rows = text_key.shape[0]
    heads = feat // DH
    group = lax.axis_size("req") // TENANTS
    place = lax.axis_index("req")
    tenant = place % TENANTS
    slot = place // TENANTS
    picker = jnp.arange(TENANTS) == tenant
    my_len = jnp.sum(jnp.where(picker, tenant_len, 0))
    my_text = jnp.sum(jnp.where(picker, text_len, 0))
    my_step = jnp.sum(jnp.where(picker, t_index, 0))
    gate_row = jnp.sum(jnp.where(picker[:, None], attn_gate, 0.0), axis=0)
    q_heads = query.reshape(tiles, heads, DH)
    cq_heads = cross_query.reshape(tiles, heads, DH)
    row_ids = jnp.arange(tiles, dtype=jnp.int32)

    def absorb(held, blocks, root):
        state, text_keys, text_values = held
        k_block, v_block, tk_block, tv_block = blocks
        valid = root * tiles + row_ids < my_len
        state = attend_block(state, q_heads, k_block, v_block, valid)
        text_keys = lax.dynamic_update_slice_in_dim(text_keys, tk_block, root * text_rows, 0)
        text_values = lax.dynamic_update_slice_in_dim(text_values, tv_block, root * text_rows, 0)
        return (state, text_keys, text_values)

    def fresh(count):
        return (
            jnp.full((heads, count), -1e30, jnp.float32),
            jnp.zeros((heads, count), jnp.float32),
            jnp.zeros((heads, count, DH), jnp.float32),
        )

    all_text = group * text_rows
    empty_text = jnp.zeros((all_text, feat), text_key.dtype)
    start_blocks = (key, value, text_key, text_value)
    held = absorb((fresh(tiles), empty_text, empty_text), start_blocks, slot)

    def turn_cycle(j, carry):
        blocks, kept = carry
        blocks = passed_along((blocks[0], blocks[1], blocks[2], blocks[3]), "req", TENANTS)
        return (blocks, absorb(kept, blocks, (slot - j) % group))

    _, held = lax.fori_loop(1, group, turn_cycle, (start_blocks, held))
    self_state, text_keys, text_values = held
    self_out = finish(self_state, tiles, feat)
    text_valid = jnp.arange(all_text, dtype=jnp.int32) < my_text
    cross_state = attend_block(fresh(tiles), cq_heads, text_keys, text_values, text_valid)
    cross_out = finish(cross_state, tiles, feat)
    self_cols = lax.all_gather(wo_self, "req", axis=1, tiled=True)
    cross_cols = lax.all_gather(wo_cross, "req", axis=1, tiled=True)
    block = gate_row[None, :] * jnp.dot(self_out, self_cols, preferred_element_type=jnp.float32)
    block = block + jnp.dot(cross_out, cross_cols, preferred_element_type=jnp.float32)
    summed = lax.psum_scatter(block.astype(jnp.bfloat16), "tp", scatter_dimension=1, tiled=True)
    valid_rows = slot * tiles + row_ids < my_len
    branch = jnp.where(valid_rows[:, None], summed, jnp.zeros((), jnp.bfloat16))
    before = shifted(branch[-1:], "req", TENANTS)
    after = shifted(branch[:1], "req", -TENANTS)
    extended = jnp.concatenate([before, branch, after], axis=0).astype(jnp.float32)
    branch32 = branch.astype(jnp.float32)
    vel = branch32 + mix_coef[None, :] * (extended[:-2] + extended[2:] - 2.0 * branch32)
    vel = jnp.where(valid_rows[:, None], vel, 0.0)
    frac = 1.0 - my_step.astype(jnp.float32) / STEPS
    sigma = 5.0 * frac / (1.0 + 4.0 * frac)
    updated = latent.astype(jnp.float32) + sigma * vel
    return (vel.astype(jnp.bfloat16), updated)


MESH = pl.DeviceIdType.MESH


def attend_head(q, k, v, count):
    scores = lax.dot_general(
        q, k, (((1,), (1,)), ((), ())), preferred_element_type=jnp.float32
    ) * (1.0 / DH**0.5)
    valid = lax.broadcasted_iota(jnp.int32, scores.shape, 1) < count
    scores = jnp.where(valid, scores, -1e30)
    top = jnp.max(scores, axis=-1, keepdims=True)
    weights = jnp.where(valid, jnp.exp(scores - top), 0.0)
    denom = jnp.sum(weights, axis=-1, keepdims=True)
    mixed = jnp.dot(weights.astype(jnp.bfloat16), v, preferred_element_type=jnp.float32)
    return (mixed / denom).astype(jnp.bfloat16)


def fused_kernel(
    group,
    len_ref,
    text_ref,
    q_in,
    k_in,
    v_in,
    cq_in,
    tk_in,
    tv_in,
    ws_in,
    wc_in,
    gate_ref,
    mix_ref,
    out,
    q_all,
    k_all,
    v_all,
    cq_all,
    tk_all,
    tv_all,
    so_all,
    co_all,
    ws_all,
    wc_all,
    mix_all,
    term,
    term_in,
    vel,
    in_send,
    in_recv,
    in_local,
    w_send,
    w_recv,
    w_local,
    mix_send,
    mix_recv,
    at_send,
    at_recv,
    term_send,
    term_recv,
    out_send,
    out_recv,
    out_local,
):
    place = lax.axis_index("req")
    y = lax.axis_index("tp")
    t = lax.rem(place, TENANTS)
    z = place // TENANTS
    half = group // 2
    tiles = q_in.shape[0]
    rows = tiles * group
    heads_here = q_in.shape[1] // (DH * group)
    sibling = t + 1 - 2 * lax.rem(t, 2)
    across = lax.rem(t + 2, TENANTS)
    other = 1 - y
    y_out = z // half
    my_len = len_ref[t]
    my_text = text_ref[t]

    def peer(k):
        return lax.rem(z + k, group)

    barrier = pltpu.get_barrier_semaphore()
    friends = [(z * TENANTS + sibling, y), (z * TENANTS + across, y), (place, other)]
    for k in range(1, group):
        friends += [(peer(k) * TENANTS + t, y), (peer(k) * TENANTS + t, other)]
    for friend in friends:
        pl.semaphore_signal(barrier, inc=1, device_id=friend, device_id_type=MESH)

    moved = [
        (q_in, q_all),
        (k_in, k_all),
        (v_in, v_all),
        (cq_in, cq_all),
        (tk_in, tk_all),
        (tv_in, tv_all),
    ]

    def own_copy(a):
        src, dst = moved[a]
        n = src.shape[0]
        width = heads_here * DH
        return pltpu.make_async_copy(
            src.at[:, pl.ds(pl.multiple_of(z * width, DH), width)],
            dst.at[pl.ds(pl.multiple_of(z * n, 16), n), :],
            in_local.at[a],
        )

    def in_copy(a, h, k):
        src, dst = moved[a]
        n = src.shape[0]
        to = peer(k)
        return pltpu.make_async_remote_copy(
            src_ref=src.at[:, pl.ds(pl.multiple_of((to * heads_here + h) * DH, DH), DH)],
            dst_ref=dst.at[
                pl.ds(pl.multiple_of(z * n, 16), n), pl.ds(pl.multiple_of(h * DH, DH), DH)
            ],
            send_sem=in_send.at[a, h, k - 1],
            recv_sem=in_recv.at[a, h, k - 1],
            device_id=(to * TENANTS + t, y),
            device_id_type=MESH,
        )

    weights = [(ws_in, ws_all), (wc_in, wc_all)]

    def w_own(i):
        src, dst = weights[i]
        return pltpu.make_async_copy(src, dst.at[t], w_local.at[i])

    def w_copy(i, hop):
        src, dst = weights[i]
        if hop == 2:
            src, block = dst.at[across], across
        else:
            block = t
        target = across if hop == 0 else sibling
        return pltpu.make_async_remote_copy(
            src_ref=src,
            dst_ref=dst.at[block],
            send_sem=w_send.at[i, hop],
            recv_sem=w_recv.at[i, hop],
            device_id=(z * TENANTS + target, y),
            device_id_type=MESH,
        )

    mix_copy = pltpu.make_async_remote_copy(
        src_ref=mix_all.at[y],
        dst_ref=mix_all.at[y],
        send_sem=mix_send,
        recv_sem=mix_recv,
        device_id=(place, other),
        device_id_type=MESH,
    )

    for a in range(6):
        own_copy(a).start()
    for i in range(2):
        w_own(i).start()
    mix_all[y] = mix_ref[...]
    for ref, filled in ((k_all, rows), (v_all, rows), (tk_all, group * tk_in.shape[0]), (tv_all, group * tv_in.shape[0])):
        if ref.shape[0] > filled:
            ref[filled:, :] = jnp.zeros((ref.shape[0] - filled, ref.shape[1]), ref.dtype)

    pl.semaphore_wait(barrier, len(friends))

    def send_head(h, carry):
        for a in range(6):
            for k in range(1, group):
                in_copy(a, h, k).start()
        return carry

    lax.fori_loop(0, heads_here, send_head, 0)
    for i in range(2):
        w_copy(i, 0).start()
    for i in range(2):
        w_copy(i, 1).start()
    mix_copy.start()
    for a in range(6):
        own_copy(a).wait()

    gathered = [so_all, co_all]

    def at_copy(i, h, k):
        column = pl.ds(pl.multiple_of((z * heads_here + h) * DH, DH), DH)
        return pltpu.make_async_remote_copy(
            src_ref=gathered[i].at[:, column],
            dst_ref=gathered[i].at[:, column],
            send_sem=at_send.at[i, h, k - 1],
            recv_sem=at_recv.at[i, h, k - 1],
            device_id=(peer(k) * TENANTS + t, y),
            device_id_type=MESH,
        )

    def do_head(h, carry):
        here = pl.ds(pl.multiple_of(h * DH, DH), DH)
        column = pl.ds(pl.multiple_of((z * heads_here + h) * DH, DH), DH)
        for i, (qr, kr, vr, count) in enumerate(
            ((q_all, k_all, v_all, my_len), (cq_all, tk_all, tv_all, my_text))
        ):
            for a in range(3 * i, 3 * i + 3):
                for k in range(1, group):
                    in_copy(a, h, k).wait_recv()
            gathered[i][:, column] = attend_head(qr[:, here], kr[:, here], vr[:, here], count)
            for k in range(1, group):
                at_copy(i, h, k).start()
        return carry

    lax.fori_loop(0, heads_here, do_head, 0)

    for i in range(2):
        w_copy(i, 0).wait_recv()
        w_copy(i, 2).start()
    for i in range(2):
        w_own(i).wait()
        w_copy(i, 1).wait_recv()
    for i in range(2):
        w_copy(i, 2).wait_recv()
    mix_copy.wait_recv()

    def wait_attended(h, carry):
        for i in range(2):
            for k in range(1, group):
                at_copy(i, h, k).wait_recv()
        return carry

    lax.fori_loop(0, heads_here, wait_attended, 0)

    def term_copy(j):
        return pltpu.make_async_remote_copy(
            src_ref=term.at[j],
            dst_ref=term_in.at[j],
            send_sem=term_send.at[j],
            recv_sem=term_recv.at[j],
            device_id=(place, other),
            device_id_type=MESH,
        )

    def project(n, carry):
        block = lax.rem(2 * other + n, TENANTS)
        total = jnp.dot(so_all[...], ws_all[block], preferred_element_type=jnp.float32)
        total = gate_ref[pl.ds(block, 1), :] * total
        total = total + jnp.dot(co_all[...], wc_all[block], preferred_element_type=jnp.float32)
        term[n] = total.astype(jnp.bfloat16)

        @pl.when(n < 2)
        def _():
            term_copy(n).start()

        return carry

    lax.fori_loop(0, TENANTS, project, 0)

    def out_block(j):
        return lax.rem(z, half) * TENANTS + 2 * y + j

    def out_copy(j, k):
        to = peer(k)
        return pltpu.make_async_remote_copy(
            src_ref=vel.at[j, pl.ds(pl.multiple_of(to * tiles, 16), tiles), :],
            dst_ref=out.at[out_block(j)],
            send_sem=out_send.at[j, k],
            recv_sem=out_recv.at[out_block(j)],
            device_id=(to * TENANTS + t, y_out),
            device_id_type=MESH,
        )

    def out_own(j):
        return pltpu.make_async_copy(
            vel.at[j, pl.ds(pl.multiple_of(z * tiles, 16), tiles), :],
            out.at[out_block(j)],
            out_local.at[j],
        )

    def smooth(j, carry):
        term_copy(j).wait_recv()
        total = term[2 + j].astype(jnp.float32) + term_in[j].astype(jnp.float32)
        branch = total.astype(jnp.bfloat16).astype(jnp.float32)
        index = lax.broadcasted_iota(jnp.int32, branch.shape, 0)
        branch = jnp.where(index < my_len, branch, 0.0)
        before = jnp.where(index == 0, 0.0, pltpu.roll(branch, 1, 0))
        after = jnp.where(index == rows - 1, 0.0, pltpu.roll(branch, rows - 1, 0))
        mix = mix_all[y_out, pl.ds(out_block(j), 1), :]
        speed = branch + mix * (before + after - 2.0 * branch)
        vel[j] = jnp.where(index < my_len, speed, 0.0).astype(jnp.bfloat16)
        for k in range(1, group):
            out_copy(j, k).start()

        @pl.when(y_out == y)
        def _():
            out_own(j).start()

        @pl.when(y_out != y)
        def _():
            out_copy(j, 0).start()

        return carry

    lax.fori_loop(0, 2, smooth, 0)

    def drain_head(h, carry):
        for k in range(1, group):
            for a in range(6):
                in_copy(a, h, k).wait_send()
            for i in range(2):
                at_copy(i, h, k).wait_send()
        return carry

    lax.fori_loop(0, heads_here, drain_head, 0)
    for i in range(2):
        for hop in range(3):
            w_copy(i, hop).wait_send()
    mix_copy.wait_send()

    def drain_out(j, carry):
        term_copy(j).wait_send()
        for k in range(1, group):
            out_copy(j, k).wait_send()

        @pl.when(y_out == y)
        def _():
            out_own(j).wait()

        @pl.when(y_out != y)
        def _():
            out_copy(j, 0).wait_send()

        return carry

    lax.fori_loop(0, 2, drain_out, 0)

    def arrive(b, carry):
        mine = jnp.logical_and(y_out == y, b // 2 == lax.rem(z, half) * 2 + y)

        @pl.when(jnp.logical_not(mine))
        def _():
            pltpu.make_async_remote_copy(
                src_ref=vel.at[0, pl.ds(0, tiles), :],
                dst_ref=out.at[b],
                send_sem=out_send.at[0, 0],
                recv_sem=out_recv.at[b],
                device_id=(place, other),
                device_id_type=MESH,
            ).wait_recv()

        return carry

    lax.fori_loop(0, out.shape[0], arrive, 0)


def fits(query, text_key, wo_self):
    group = lax.axis_size("req") // TENANTS
    heads = query.shape[1] // DH
    return (
        lax.axis_size("tp") == 2
        and group >= 2
        and group % 2 == 0
        and heads % group == 0
        and query.shape[0] % 16 == 0
        and text_key.shape[0] % 16 == 0
        and wo_self.shape[0] == query.shape[1]
    )


def by_heads(
    query,
    key,
    value,
    cross_query,
    text_key,
    text_value,
    wo_self,
    wo_cross,
    attn_gate,
    mix_coef,
    latent,
    tenant_len,
    text_len,
    t_index,
):
    tiles, feat = query.shape
    text_rows = text_key.shape[0]
    blocks = lax.axis_size("req")
    group = blocks // TENANTS
    cols = wo_self.shape[1]
    heads_here = feat // DH // group
    width = heads_here * DH
    rows = tiles * group
    padded = -(-rows // 128) * 128
    texts = -(-text_rows * group // 128) * 128
    place = lax.axis_index("req")
    tenant = place % TENANTS
    slot = place // TENANTS
    gate = lax.dynamic_slice(attn_gate, (tenant, slot * TENANTS * cols), (1, TENANTS * cols))
    gate = gate.reshape(TENANTS, cols)
    mix = mix_coef.reshape(blocks // 2, cols)
    bf = jnp.bfloat16
    dma = pltpu.SemaphoreType.DMA
    any_spec = pl.BlockSpec(memory_space=pl.ANY)
    smem = pl.BlockSpec(memory_space=pltpu.SMEM)
    vmem = pl.BlockSpec(memory_space=pltpu.VMEM)
    flops = 4 * rows * width * (padded + texts) + 4 * rows * feat * TENANTS * cols
    moved = pl.pallas_call(
        functools.partial(fused_kernel, group),
        out_shape=jax.ShapeDtypeStruct((blocks // 2, tiles, cols), bf),
        in_specs=[smem, smem] + [any_spec] * 8 + [vmem, vmem],
        out_specs=any_spec,
        scratch_shapes=[
            pltpu.VMEM((rows, width), bf),
            pltpu.VMEM((padded, width), bf),
            pltpu.VMEM((padded, width), bf),
            pltpu.VMEM((rows, width), bf),
            pltpu.VMEM((texts, width), bf),
            pltpu.VMEM((texts, width), bf),
            pltpu.VMEM((rows, feat), bf),
            pltpu.VMEM((rows, feat), bf),
            pltpu.VMEM((TENANTS, feat, cols), bf),
            pltpu.VMEM((TENANTS, feat, cols), bf),
            pltpu.VMEM((2, blocks // 2, cols), jnp.float32),
            pltpu.VMEM((TENANTS, rows, cols), bf),
            pltpu.VMEM((2, rows, cols), bf),
            pltpu.VMEM((2, rows, cols), bf),
            dma((6, heads_here, group - 1)),
            dma((6, heads_here, group - 1)),
            dma((6,)),
            dma((2, 3)),
            dma((2, 3)),
            dma((2,)),
            dma,
            dma,
            dma((2, heads_here, group - 1)),
            dma((2, heads_here, group - 1)),
            dma((2,)),
            dma((2,)),
            dma((2, group)),
            dma((blocks // 2,)),
            dma((2,)),
        ],
        compiler_params=pltpu.CompilerParams(
            collective_id=0, has_side_effects=True, vmem_limit_bytes=48 * 1024 * 1024
        ),
        cost_estimate=pl.CostEstimate(
            flops=flops, bytes_accessed=16 * feat * cols, transcendentals=rows * heads_here * (padded + texts)
        ),
        name="attend_project",
    )(
        tenant_len,
        text_len,
        query,
        key,
        value,
        cross_query,
        text_key,
        text_value,
        wo_self,
        wo_cross,
        gate,
        mix,
    )
    velocity = moved.transpose(1, 0, 2).reshape(tiles, blocks // 2 * cols)
    step = jnp.sum(jnp.where(jnp.arange(TENANTS) == tenant, t_index, 0))
    frac = 1.0 - step.astype(jnp.float32) / STEPS
    sigma = 5.0 * frac / (1.0 + 4.0 * frac)
    return (velocity, latent.astype(jnp.float32) + sigma * velocity.astype(jnp.float32))


def either(*arrays):
    if fits(arrays[0], arrays[4], arrays[6]):
        return by_heads(*arrays)
    return shards(*arrays)


def solution(mesh):
    placed = (
        P("req", "tp"),
        P("req", "tp"),
        P("req", "tp"),
        P("req", "tp"),
        P("req", "tp"),
        P("req", "tp"),
        P("tp", "req"),
        P("tp", "req"),
        P(),
        P("tp"),
        P("req", "tp"),
        P(),
        P(),
        P(),
    )
    return jax.shard_map(
        either,
        mesh=mesh,
        in_specs=placed,
        out_specs=(P("req", "tp"), P("req", "tp")),
        check_vma=False,
    )
```

```python
import functools

import jax
import jax.numpy as jnp
from jax import lax
from jax.experimental import pallas as pl
from jax.experimental.pallas import tpu as pltpu
from jax.sharding import PartitionSpec as P

DH = 128
TENANTS = 4
STEPS = 50


def passed_along(block, axis, distance):
    devices = range(lax.axis_size(axis))
    route = [((i - distance) % len(devices), i) for i in devices]
    return lax.ppermute(block, axis, route)


def shifted(block, axis, distance):
    devices = range(lax.axis_size(axis))
    route = [(i - distance, i) for i in devices if i - distance in devices]
    return lax.ppermute(block, axis, route)


def attend_block(state, q_heads, k_block, v_block, valid):
    top, denom, accum = state
    heads = q_heads.shape[1]
    k_heads = k_block.reshape(k_block.shape[0], heads, DH)
    v_heads = v_block.reshape(v_block.shape[0], heads, DH)
    scores = jnp.einsum("qhd,khd->hqk", q_heads, k_heads, preferred_element_type=jnp.float32) * (
        1.0 / DH**0.5
    )
    scores = jnp.where(valid[None, None, :], scores, -1e30)
    new_top = jnp.maximum(top, jnp.max(scores, axis=-1))
    weights = jnp.where(valid[None, None, :], jnp.exp(scores - new_top[..., None]), 0.0)
    factor = jnp.exp(top - new_top)
    denom = denom * factor + jnp.sum(weights, axis=-1)
    mixed = jnp.einsum(
        "hqk,khd->hqd", weights.astype(jnp.bfloat16), v_heads, preferred_element_type=jnp.float32
    )
    return (new_top, denom, accum * factor[..., None] + mixed)


def finish(state, tiles, feat):
    top, denom, accum = state
    out = accum / denom[..., None]
    return out.transpose(1, 0, 2).reshape(tiles, feat).astype(jnp.bfloat16)


def shards(
    query,
    key,
    value,
    cross_query,
    text_key,
    text_value,
    wo_self,
    wo_cross,
    attn_gate,
    mix_coef,
    latent,
    tenant_len,
    text_len,
    t_index,
):
    tiles, feat = query.shape
    text_rows = text_key.shape[0]
    heads = feat // DH
    group = lax.axis_size("req") // TENANTS
    place = lax.axis_index("req")
    tenant = place % TENANTS
    slot = place // TENANTS
    picker = jnp.arange(TENANTS) == tenant
    my_len = jnp.sum(jnp.where(picker, tenant_len, 0))
    my_text = jnp.sum(jnp.where(picker, text_len, 0))
    my_step = jnp.sum(jnp.where(picker, t_index, 0))
    gate_row = jnp.sum(jnp.where(picker[:, None], attn_gate, 0.0), axis=0)
    q_heads = query.reshape(tiles, heads, DH)
    cq_heads = cross_query.reshape(tiles, heads, DH)
    row_ids = jnp.arange(tiles, dtype=jnp.int32)

    def absorb(held, blocks, root):
        state, text_keys, text_values = held
        k_block, v_block, tk_block, tv_block = blocks
        valid = root * tiles + row_ids < my_len
        state = attend_block(state, q_heads, k_block, v_block, valid)
        text_keys = lax.dynamic_update_slice_in_dim(text_keys, tk_block, root * text_rows, 0)
        text_values = lax.dynamic_update_slice_in_dim(text_values, tv_block, root * text_rows, 0)
        return (state, text_keys, text_values)

    def fresh(count):
        return (
            jnp.full((heads, count), -1e30, jnp.float32),
            jnp.zeros((heads, count), jnp.float32),
            jnp.zeros((heads, count, DH), jnp.float32),
        )

    all_text = group * text_rows
    empty_text = jnp.zeros((all_text, feat), text_key.dtype)
    start_blocks = (key, value, text_key, text_value)
    held = absorb((fresh(tiles), empty_text, empty_text), start_blocks, slot)

    def turn_cycle(j, carry):
        blocks, kept = carry
        blocks = passed_along((blocks[0], blocks[1], blocks[2], blocks[3]), "req", TENANTS)
        return (blocks, absorb(kept, blocks, (slot - j) % group))

    _, held = lax.fori_loop(1, group, turn_cycle, (start_blocks, held))
    self_state, text_keys, text_values = held
    self_out = finish(self_state, tiles, feat)
    text_valid = jnp.arange(all_text, dtype=jnp.int32) < my_text
    cross_state = attend_block(fresh(tiles), cq_heads, text_keys, text_values, text_valid)
    cross_out = finish(cross_state, tiles, feat)
    self_cols = lax.all_gather(wo_self, "req", axis=1, tiled=True)
    cross_cols = lax.all_gather(wo_cross, "req", axis=1, tiled=True)
    block = gate_row[None, :] * jnp.dot(self_out, self_cols, preferred_element_type=jnp.float32)
    block = block + jnp.dot(cross_out, cross_cols, preferred_element_type=jnp.float32)
    summed = lax.psum_scatter(block.astype(jnp.bfloat16), "tp", scatter_dimension=1, tiled=True)
    valid_rows = slot * tiles + row_ids < my_len
    branch = jnp.where(valid_rows[:, None], summed, jnp.zeros((), jnp.bfloat16))
    before = shifted(branch[-1:], "req", TENANTS)
    after = shifted(branch[:1], "req", -TENANTS)
    extended = jnp.concatenate([before, branch, after], axis=0).astype(jnp.float32)
    branch32 = branch.astype(jnp.float32)
    vel = branch32 + mix_coef[None, :] * (extended[:-2] + extended[2:] - 2.0 * branch32)
    vel = jnp.where(valid_rows[:, None], vel, 0.0)
    frac = 1.0 - my_step.astype(jnp.float32) / STEPS
    sigma = 5.0 * frac / (1.0 + 4.0 * frac)
    updated = latent.astype(jnp.float32) + sigma * vel
    return (vel.astype(jnp.bfloat16), updated)


MESH = pl.DeviceIdType.MESH


def attend_head(q, k, v, count):
    scores = lax.dot_general(
        q, k, (((1,), (1,)), ((), ())), preferred_element_type=jnp.float32
    ) * (1.0 / DH**0.5)
    valid = lax.broadcasted_iota(jnp.int32, scores.shape, 1) < count
    scores = jnp.where(valid, scores, -1e30)
    top = jnp.max(scores, axis=-1, keepdims=True)
    weights = jnp.where(valid, jnp.exp(scores - top), 0.0)
    denom = jnp.sum(weights, axis=-1, keepdims=True)
    mixed = jnp.dot(weights.astype(jnp.bfloat16), v, preferred_element_type=jnp.float32)
    return (mixed / denom).astype(jnp.bfloat16)


def fused_kernel(
    group,
    len_ref,
    text_ref,
    q_in,
    k_in,
    v_in,
    cq_in,
    tk_in,
    tv_in,
    ws_in,
    wc_in,
    gate_ref,
    mix_ref,
    out,
    q_all,
    k_all,
    v_all,
    cq_all,
    tk_all,
    tv_all,
    so_all,
    co_all,
    ws_all,
    wc_all,
    mix_all,
    term,
    term_own,
    term_in,
    vel,
    in_send,
    in_recv,
    in_local,
    w_send,
    w_recv,
    w_local,
    mix_send,
    mix_recv,
    at_send,
    at_recv,
    term_send,
    term_recv,
    out_send,
    out_recv,
    out_local,
):
    place = lax.axis_index("req")
    y = lax.axis_index("tp")
    t = lax.rem(place, TENANTS)
    z = place // TENANTS
    half = group // 2
    tiles = q_in.shape[0]
    rows = tiles * group
    heads_here = q_in.shape[1] // (DH * group)
    sibling = t + 1 - 2 * lax.rem(t, 2)
    across = lax.rem(t + 2, TENANTS)
    other = 1 - y
    y_out = z // half
    my_len = len_ref[t]
    my_text = text_ref[t]

    def peer(k):
        return lax.rem(z + k, group)

    barrier = pltpu.get_barrier_semaphore()
    friends = [(z * TENANTS + sibling, y), (z * TENANTS + across, y), (place, other)]
    for k in range(1, group):
        friends += [(peer(k) * TENANTS + t, y), (peer(k) * TENANTS + t, other)]
    for friend in friends:
        pl.semaphore_signal(barrier, inc=1, device_id=friend, device_id_type=MESH)

    moved = [
        (q_in, q_all),
        (k_in, k_all),
        (v_in, v_all),
        (cq_in, cq_all),
        (tk_in, tk_all),
        (tv_in, tv_all),
    ]

    def own_copy(a):
        src, dst = moved[a]
        n = src.shape[0]
        width = heads_here * DH
        return pltpu.make_async_copy(
            src.at[:, pl.ds(pl.multiple_of(z * width, DH), width)],
            dst.at[pl.ds(pl.multiple_of(z * n, 16), n), :],
            in_local.at[a],
        )

    def in_copy(a, h, k):
        src, dst = moved[a]
        n = src.shape[0]
        to = peer(k)
        return pltpu.make_async_remote_copy(
            src_ref=src.at[:, pl.ds(pl.multiple_of((to * heads_here + h) * DH, DH), DH)],
            dst_ref=dst.at[
                pl.ds(pl.multiple_of(z * n, 16), n), pl.ds(pl.multiple_of(h * DH, DH), DH)
            ],
            send_sem=in_send.at[a, h, k - 1],
            recv_sem=in_recv.at[a, h, k - 1],
            device_id=(to * TENANTS + t, y),
            device_id_type=MESH,
        )

    weights = [(ws_in, ws_all), (wc_in, wc_all)]

    cols = ws_in.shape[0]

    def w_rows(block):
        return pl.ds(pl.multiple_of(block * cols, 16), cols)

    def w_own(i):
        src, dst = weights[i]
        return pltpu.make_async_copy(src, dst.at[w_rows(t), :], w_local.at[i])

    def w_copy(i, hop):
        src, dst = weights[i]
        if hop == 2:
            src, block = dst.at[w_rows(across), :], across
        else:
            block = t
        target = across if hop == 0 else sibling
        return pltpu.make_async_remote_copy(
            src_ref=src,
            dst_ref=dst.at[w_rows(block), :],
            send_sem=w_send.at[i, hop],
            recv_sem=w_recv.at[i, hop],
            device_id=(z * TENANTS + target, y),
            device_id_type=MESH,
        )

    mix_copy = pltpu.make_async_remote_copy(
        src_ref=mix_all.at[y],
        dst_ref=mix_all.at[y],
        send_sem=mix_send,
        recv_sem=mix_recv,
        device_id=(place, other),
        device_id_type=MESH,
    )

    for a in range(6):
        own_copy(a).start()
    for i in range(2):
        w_own(i).start()
    mix_all[y] = mix_ref[...]
    for ref, filled in ((k_all, rows), (v_all, rows), (tk_all, group * tk_in.shape[0]), (tv_all, group * tv_in.shape[0])):
        if ref.shape[0] > filled:
            ref[filled:, :] = jnp.zeros((ref.shape[0] - filled, ref.shape[1]), ref.dtype)

    pl.semaphore_wait(barrier, len(friends))

    def send_half(h, i):
        for a in range(3 * i, 3 * i + 3):
            for k in range(group - 1, 0, -1):
                in_copy(a, h, k).start()

    send_half(0, 0)
    send_half(0, 1)
    for i in range(2):
        w_copy(i, 0).start()
    for i in range(2):
        w_copy(i, 1).start()
    mix_copy.start()
    for a in range(6):
        own_copy(a).wait()

    gathered = [so_all, co_all]

    def at_copy(i, h, k):
        column = pl.ds(pl.multiple_of((z * heads_here + h) * DH, DH), DH)
        return pltpu.make_async_remote_copy(
            src_ref=gathered[i].at[:, column],
            dst_ref=gathered[i].at[:, column],
            send_sem=at_send.at[i, h, k - 1],
            recv_sem=at_recv.at[i, h, k - 1],
            device_id=(peer(k) * TENANTS + t, y),
            device_id_type=MESH,
        )

    def do_head(h, carry):
        here = pl.ds(pl.multiple_of(h * DH, DH), DH)
        column = pl.ds(pl.multiple_of((z * heads_here + h) * DH, DH), DH)
        for i, (qr, kr, vr, count) in enumerate(
            ((q_all, k_all, v_all, my_len), (cq_all, tk_all, tv_all, my_text))
        ):
            for a in range(3 * i, 3 * i + 3):
                for k in range(1, group):
                    in_copy(a, h, k).wait_recv()

            @pl.when(h + 1 < heads_here)
            def _():
                send_half(h + 1, i)

            gathered[i][:, column] = attend_head(qr[:, here], kr[:, here], vr[:, here], count)
            for k in range(1, group):
                at_copy(i, h, k).start()
        return carry

    lax.fori_loop(0, heads_here, do_head, 0)

    for i in range(2):
        w_copy(i, 0).wait_recv()
        w_copy(i, 2).start()
    for i in range(2):
        w_own(i).wait()
        w_copy(i, 1).wait_recv()
    for i in range(2):
        w_copy(i, 2).wait_recv()
    mix_copy.wait_recv()

    def wait_attended(h, carry):
        for i in range(2):
            for k in range(1, group):
                at_copy(i, h, k).wait_recv()
        return carry

    lax.fori_loop(0, heads_here, wait_attended, 0)

    side = term.shape[1]
    chunks = [(at, min(256, side - at)) for at in range(0, side, 256)]

    def term_copy(j):
        at, n = chunks[j]
        return pltpu.make_async_remote_copy(
            src_ref=term.at[:, pl.ds(at, n)],
            dst_ref=term_in.at[:, pl.ds(at, n)],
            send_sem=term_send.at[j],
            recv_sem=term_recv.at[j],
            device_id=(place, other),
            device_id_type=MESH,
        )

    def project(whose, j):
        at, n = chunks[j]
        start = pl.multiple_of(whose * side + at, 128)
        across_rows = (((1,), (1,)), ((), ()))
        total = lax.dot_general(
            so_all[...], ws_all[pl.ds(start, n), :], across_rows, preferred_element_type=jnp.float32
        )
        first = pl.multiple_of(z * (2 * side) + whose * side + at, 128)
        gates = gate_ref[:, pl.ds(first, n)]
        mine = lax.broadcasted_iota(jnp.int32, gates.shape, 0) == t
        total = jnp.sum(jnp.where(mine, gates, 0.0), axis=0, keepdims=True) * total
        total = total + lax.dot_general(
            co_all[...], wc_all[pl.ds(start, n), :], across_rows, preferred_element_type=jnp.float32
        )
        return total.astype(jnp.bfloat16)

    for j, (at, n) in enumerate(chunks):
        term[:, at : at + n] = project(other, j)
        term_copy(j).start()
    for j, (at, n) in enumerate(chunks):
        term_own[:, at : at + n] = project(y, j)

    source = lax.rem(z, half) * 2 + y

    def out_columns(sender, j):
        at, n = chunks[j]
        return pl.ds(pl.multiple_of(sender * side + at, 128), n)

    def vel_part(j, to):
        at, n = chunks[j]
        return vel.at[pl.ds(pl.multiple_of(to * tiles, 16), tiles), pl.ds(at, n)]

    def out_copy(j, k):
        to = peer(k)
        return pltpu.make_async_remote_copy(
            src_ref=vel_part(j, to),
            dst_ref=out.at[:, out_columns(source, j)],
            send_sem=out_send.at[j, k],
            recv_sem=out_recv.at[source, j],
            device_id=(to * TENANTS + t, y_out),
            device_id_type=MESH,
        )

    def out_own(j):
        return pltpu.make_async_copy(
            vel_part(j, z), out.at[:, out_columns(source, j)], out_local.at[j]
        )

    for j, (at, n) in enumerate(chunks):
        term_copy(j).wait_recv()
        total = term_own[:, at : at + n].astype(jnp.float32)
        total = total + term_in[:, at : at + n].astype(jnp.float32)
        branch = total.astype(jnp.bfloat16).astype(jnp.float32)
        index = lax.broadcasted_iota(jnp.int32, branch.shape, 0)
        branch = jnp.where(index < my_len, branch, 0.0)
        before = jnp.where(index == 0, 0.0, pltpu.roll(branch, 1, 0))
        after = jnp.where(index == rows - 1, 0.0, pltpu.roll(branch, rows - 1, 0))
        mix = mix_all[y_out, :, out_columns(source, j)]
        speed = branch + mix * (before + after - 2.0 * branch)
        vel[:, at : at + n] = jnp.where(index < my_len, speed, 0.0).astype(jnp.bfloat16)
        for k in range(group - 1, 0, -1):
            out_copy(j, k).start()

        @pl.when(y_out == y)
        def _():
            out_own(j).start()

        @pl.when(y_out != y)
        def _():
            out_copy(j, 0).start()

    def drain_head(h, carry):
        for k in range(1, group):
            for a in range(6):
                in_copy(a, h, k).wait_send()
            for i in range(2):
                at_copy(i, h, k).wait_send()
        return carry

    lax.fori_loop(0, heads_here, drain_head, 0)
    for i in range(2):
        for hop in range(3):
            w_copy(i, hop).wait_send()
    mix_copy.wait_send()

    for j in range(len(chunks)):
        term_copy(j).wait_send()
        for k in range(1, group):
            out_copy(j, k).wait_send()

        @pl.when(y_out == y)
        def _():
            out_own(j).wait()

        @pl.when(y_out != y)
        def _():
            out_copy(j, 0).wait_send()

    def arrive(sender, carry):
        mine = jnp.logical_and(y_out == y, sender == source)

        @pl.when(jnp.logical_not(mine))
        def _():
            for j in range(len(chunks)):
                pltpu.make_async_remote_copy(
                    src_ref=vel_part(j, 0),
                    dst_ref=out.at[:, out_columns(sender, j)],
                    send_sem=out_send.at[j, 0],
                    recv_sem=out_recv.at[sender, j],
                    device_id=(place, other),
                    device_id_type=MESH,
                ).wait_recv()

        return carry

    lax.fori_loop(0, group, arrive, 0)


def fits(query, text_key, wo_self):
    group = lax.axis_size("req") // TENANTS
    heads = query.shape[1] // DH
    return (
        lax.axis_size("tp") == 2
        and group >= 2
        and group % 2 == 0
        and heads % group == 0
        and query.shape[0] % 16 == 0
        and text_key.shape[0] % 16 == 0
        and wo_self.shape[0] == query.shape[1]
        and wo_self.shape[1] % 64 == 0
    )


def by_heads(
    query,
    key,
    value,
    cross_query,
    text_key,
    text_value,
    wo_self,
    wo_cross,
    attn_gate,
    mix_coef,
    latent,
    tenant_len,
    text_len,
    t_index,
):
    tiles, feat = query.shape
    text_rows = text_key.shape[0]
    blocks = lax.axis_size("req")
    group = blocks // TENANTS
    cols = wo_self.shape[1]
    heads_here = feat // DH // group
    width = heads_here * DH
    rows = tiles * group
    padded = -(-rows // 128) * 128
    texts = -(-text_rows * group // 128) * 128
    place = lax.axis_index("req")
    tenant = place % TENANTS
    slot = place // TENANTS
    side = cols * TENANTS // 2
    chunks = -(-side // 256)
    mix = mix_coef.reshape(1, -1)
    bf = jnp.bfloat16
    dma = pltpu.SemaphoreType.DMA
    any_spec = pl.BlockSpec(memory_space=pltpu.HBM)
    smem = pl.BlockSpec(memory_space=pltpu.SMEM)
    vmem = pl.BlockSpec(memory_space=pltpu.VMEM)
    flops = 4 * rows * width * (padded + texts) + 4 * rows * feat * TENANTS * cols
    velocity = pl.pallas_call(
        functools.partial(fused_kernel, group),
        out_shape=jax.ShapeDtypeStruct((tiles, blocks // 2 * cols), bf),
        in_specs=[smem, smem] + [any_spec] * 8 + [vmem, vmem],
        out_specs=any_spec,
        scratch_shapes=[
            pltpu.VMEM((rows, width), bf),
            pltpu.VMEM((padded, width), bf),
            pltpu.VMEM((padded, width), bf),
            pltpu.VMEM((rows, width), bf),
            pltpu.VMEM((texts, width), bf),
            pltpu.VMEM((texts, width), bf),
            pltpu.VMEM((rows, feat), bf),
            pltpu.VMEM((rows, feat), bf),
            pltpu.VMEM((TENANTS * cols, feat), bf),
            pltpu.VMEM((TENANTS * cols, feat), bf),
            pltpu.VMEM((2, 1, blocks // 2 * cols), jnp.float32),
            pltpu.VMEM((rows, side), bf),
            pltpu.VMEM((rows, side), bf),
            pltpu.VMEM((rows, side), bf),
            pltpu.VMEM((rows, side), bf),
            dma((6, heads_here, group - 1)),
            dma((6, heads_here, group - 1)),
            dma((6,)),
            dma((2, 3)),
            dma((2, 3)),
            dma((2,)),
            dma,
            dma,
            dma((2, heads_here, group - 1)),
            dma((2, heads_here, group - 1)),
            dma((chunks,)),
            dma((chunks,)),
            dma((chunks, group)),
            dma((group, chunks)),
            dma((chunks,)),
        ],
        compiler_params=pltpu.CompilerParams(
            collective_id=0, has_side_effects=True, vmem_limit_bytes=60 * 1024 * 1024
        ),
        cost_estimate=pl.CostEstimate(
            flops=flops, bytes_accessed=16 * feat * cols, transcendentals=rows * heads_here * (padded + texts)
        ),
        name="attend_project",
    )(
        tenant_len,
        text_len,
        query,
        key,
        value,
        cross_query,
        text_key,
        text_value,
        wo_self.T,
        wo_cross.T,
        attn_gate,
        mix,
    )
    step = jnp.sum(jnp.where(jnp.arange(TENANTS) == tenant, t_index, 0))
    frac = 1.0 - step.astype(jnp.float32) / STEPS
    sigma = 5.0 * frac / (1.0 + 4.0 * frac)
    return (velocity, latent.astype(jnp.float32) + sigma * velocity.astype(jnp.float32))


def either(*arrays):
    if fits(arrays[0], arrays[4], arrays[6]):
        return by_heads(*arrays)
    return shards(*arrays)


def solution(mesh):
    placed = (
        P("req", "tp"),
        P("req", "tp"),
        P("req", "tp"),
        P("req", "tp"),
        P("req", "tp"),
        P("req", "tp"),
        P("tp", "req"),
        P("tp", "req"),
        P(),
        P("tp"),
        P("req", "tp"),
        P(),
        P(),
        P(),
    )
    return jax.shard_map(
        either,
        mesh=mesh,
        in_specs=placed,
        out_specs=(P("req", "tp"), P("req", "tp")),
        check_vma=False,
    )
```

```python
import functools

import jax
import jax.numpy as jnp
from jax import lax
from jax.experimental import pallas as pl
from jax.experimental.pallas import tpu as pltpu
from jax.sharding import PartitionSpec as P

DH = 128
TENANTS = 4
STEPS = 50


def passed_along(block, axis, distance):
    devices = range(lax.axis_size(axis))
    route = [((i - distance) % len(devices), i) for i in devices]
    return lax.ppermute(block, axis, route)


def shifted(block, axis, distance):
    devices = range(lax.axis_size(axis))
    route = [(i - distance, i) for i in devices if i - distance in devices]
    return lax.ppermute(block, axis, route)


def attend_block(state, q_heads, k_block, v_block, valid):
    top, denom, accum = state
    heads = q_heads.shape[1]
    k_heads = k_block.reshape(k_block.shape[0], heads, DH)
    v_heads = v_block.reshape(v_block.shape[0], heads, DH)
    scores = jnp.einsum("qhd,khd->hqk", q_heads, k_heads, preferred_element_type=jnp.float32) * (
        1.0 / DH**0.5
    )
    scores = jnp.where(valid[None, None, :], scores, -1e30)
    new_top = jnp.maximum(top, jnp.max(scores, axis=-1))
    weights = jnp.where(valid[None, None, :], jnp.exp(scores - new_top[..., None]), 0.0)
    factor = jnp.exp(top - new_top)
    denom = denom * factor + jnp.sum(weights, axis=-1)
    mixed = jnp.einsum(
        "hqk,khd->hqd", weights.astype(jnp.bfloat16), v_heads, preferred_element_type=jnp.float32
    )
    return (new_top, denom, accum * factor[..., None] + mixed)


def finish(state, tiles, feat):
    top, denom, accum = state
    out = accum / denom[..., None]
    return out.transpose(1, 0, 2).reshape(tiles, feat).astype(jnp.bfloat16)


def shards(
    query,
    key,
    value,
    cross_query,
    text_key,
    text_value,
    wo_self,
    wo_cross,
    attn_gate,
    mix_coef,
    latent,
    tenant_len,
    text_len,
    t_index,
):
    tiles, feat = query.shape
    text_rows = text_key.shape[0]
    heads = feat // DH
    group = lax.axis_size("req") // TENANTS
    place = lax.axis_index("req")
    tenant = place % TENANTS
    slot = place // TENANTS
    picker = jnp.arange(TENANTS) == tenant
    my_len = jnp.sum(jnp.where(picker, tenant_len, 0))
    my_text = jnp.sum(jnp.where(picker, text_len, 0))
    my_step = jnp.sum(jnp.where(picker, t_index, 0))
    gate_row = jnp.sum(jnp.where(picker[:, None], attn_gate, 0.0), axis=0)
    q_heads = query.reshape(tiles, heads, DH)
    cq_heads = cross_query.reshape(tiles, heads, DH)
    row_ids = jnp.arange(tiles, dtype=jnp.int32)

    def absorb(held, blocks, root):
        state, text_keys, text_values = held
        k_block, v_block, tk_block, tv_block = blocks
        valid = root * tiles + row_ids < my_len
        state = attend_block(state, q_heads, k_block, v_block, valid)
        text_keys = lax.dynamic_update_slice_in_dim(text_keys, tk_block, root * text_rows, 0)
        text_values = lax.dynamic_update_slice_in_dim(text_values, tv_block, root * text_rows, 0)
        return (state, text_keys, text_values)

    def fresh(count):
        return (
            jnp.full((heads, count), -1e30, jnp.float32),
            jnp.zeros((heads, count), jnp.float32),
            jnp.zeros((heads, count, DH), jnp.float32),
        )

    all_text = group * text_rows
    empty_text = jnp.zeros((all_text, feat), text_key.dtype)
    start_blocks = (key, value, text_key, text_value)
    held = absorb((fresh(tiles), empty_text, empty_text), start_blocks, slot)

    def turn_cycle(j, carry):
        blocks, kept = carry
        blocks = passed_along((blocks[0], blocks[1], blocks[2], blocks[3]), "req", TENANTS)
        return (blocks, absorb(kept, blocks, (slot - j) % group))

    _, held = lax.fori_loop(1, group, turn_cycle, (start_blocks, held))
    self_state, text_keys, text_values = held
    self_out = finish(self_state, tiles, feat)
    text_valid = jnp.arange(all_text, dtype=jnp.int32) < my_text
    cross_state = attend_block(fresh(tiles), cq_heads, text_keys, text_values, text_valid)
    cross_out = finish(cross_state, tiles, feat)
    self_cols = lax.all_gather(wo_self, "req", axis=1, tiled=True)
    cross_cols = lax.all_gather(wo_cross, "req", axis=1, tiled=True)
    block = gate_row[None, :] * jnp.dot(self_out, self_cols, preferred_element_type=jnp.float32)
    block = block + jnp.dot(cross_out, cross_cols, preferred_element_type=jnp.float32)
    summed = lax.psum_scatter(block.astype(jnp.bfloat16), "tp", scatter_dimension=1, tiled=True)
    valid_rows = slot * tiles + row_ids < my_len
    branch = jnp.where(valid_rows[:, None], summed, jnp.zeros((), jnp.bfloat16))
    before = shifted(branch[-1:], "req", TENANTS)
    after = shifted(branch[:1], "req", -TENANTS)
    extended = jnp.concatenate([before, branch, after], axis=0).astype(jnp.float32)
    branch32 = branch.astype(jnp.float32)
    vel = branch32 + mix_coef[None, :] * (extended[:-2] + extended[2:] - 2.0 * branch32)
    vel = jnp.where(valid_rows[:, None], vel, 0.0)
    frac = 1.0 - my_step.astype(jnp.float32) / STEPS
    sigma = 5.0 * frac / (1.0 + 4.0 * frac)
    updated = latent.astype(jnp.float32) + sigma * vel
    return (vel.astype(jnp.bfloat16), updated)


MESH = pl.DeviceIdType.MESH


def attend_head(q, k, v, count):
    scores = lax.dot_general(
        q, k, (((1,), (1,)), ((), ())), preferred_element_type=jnp.float32
    ) * (1.0 / DH**0.5)
    valid = lax.broadcasted_iota(jnp.int32, scores.shape, 1) < count
    scores = jnp.where(valid, scores, -1e30)
    top = jnp.max(scores, axis=-1, keepdims=True)
    weights = jnp.where(valid, jnp.exp(scores - top), 0.0)
    denom = jnp.sum(weights, axis=-1, keepdims=True)
    mixed = jnp.dot(weights.astype(jnp.bfloat16), v, preferred_element_type=jnp.float32)
    return (mixed / denom).astype(jnp.bfloat16)


def fused_kernel(
    group,
    len_ref,
    text_ref,
    q_in,
    k_in,
    v_in,
    cq_in,
    tk_in,
    tv_in,
    ws_in,
    wc_in,
    gate_ref,
    mix_ref,
    out,
    q_all,
    k_all,
    v_all,
    cq_all,
    tk_all,
    tv_all,
    so_all,
    co_all,
    ws_all,
    wc_all,
    mix_all,
    term,
    term_own,
    term_in,
    vel,
    in_send,
    in_recv,
    in_local,
    w_send,
    w_recv,
    w_local,
    mix_send,
    mix_recv,
    at_send,
    at_recv,
    term_send,
    term_recv,
    out_send,
    out_recv,
    out_local,
):
    place = lax.axis_index("req")
    y = lax.axis_index("tp")
    t = lax.rem(place, TENANTS)
    z = place // TENANTS
    half = group // 2
    tiles = q_in.shape[0]
    rows = tiles * group
    heads_here = q_in.shape[1] // (DH * group)
    sibling = t + 1 - 2 * lax.rem(t, 2)
    across = lax.rem(t + 2, TENANTS)
    other = 1 - y
    y_out = z // half
    my_len = len_ref[t]
    my_text = text_ref[t]

    def peer(k):
        return lax.rem(z + k, group)

    barrier = pltpu.get_barrier_semaphore()
    friends = [(z * TENANTS + sibling, y), (z * TENANTS + across, y), (place, other)]
    for k in range(1, group):
        friends += [(peer(k) * TENANTS + t, y), (peer(k) * TENANTS + t, other)]
    for friend in friends:
        pl.semaphore_signal(barrier, inc=1, device_id=friend, device_id_type=MESH)

    moved = [
        (q_in, q_all),
        (k_in, k_all),
        (v_in, v_all),
        (cq_in, cq_all),
        (tk_in, tk_all),
        (tv_in, tv_all),
    ]

    def own_copy(a):
        src, dst = moved[a]
        n = src.shape[0]
        width = heads_here * DH
        return pltpu.make_async_copy(
            src.at[:, pl.ds(pl.multiple_of(z * width, DH), width)],
            dst.at[pl.ds(pl.multiple_of(z * n, 16), n), :],
            in_local.at[a],
        )

    def in_copy(a, h, k):
        src, dst = moved[a]
        n = src.shape[0]
        to = peer(k)
        return pltpu.make_async_remote_copy(
            src_ref=src.at[:, pl.ds(pl.multiple_of((to * heads_here + h) * DH, DH), DH)],
            dst_ref=dst.at[
                pl.ds(pl.multiple_of(z * n, 16), n), pl.ds(pl.multiple_of(h * DH, DH), DH)
            ],
            send_sem=in_send.at[a, h, k - 1],
            recv_sem=in_recv.at[a, h, k - 1],
            device_id=(to * TENANTS + t, y),
            device_id_type=MESH,
        )

    weights = [(ws_in, ws_all), (wc_in, wc_all)]

    cols = ws_in.shape[0]

    def w_rows(block):
        return pl.ds(pl.multiple_of(block * cols, 16), cols)

    def w_own(i):
        src, dst = weights[i]
        return pltpu.make_async_copy(src, dst.at[w_rows(t), :], w_local.at[i])

    def w_copy(i, hop):
        src, dst = weights[i]
        if hop == 2:
            src, block = dst.at[w_rows(across), :], across
        else:
            block = t
        target = across if hop == 0 else sibling
        return pltpu.make_async_remote_copy(
            src_ref=src,
            dst_ref=dst.at[w_rows(block), :],
            send_sem=w_send.at[i, hop],
            recv_sem=w_recv.at[i, hop],
            device_id=(z * TENANTS + target, y),
            device_id_type=MESH,
        )

    mix_copy = pltpu.make_async_remote_copy(
        src_ref=mix_all.at[y],
        dst_ref=mix_all.at[y],
        send_sem=mix_send,
        recv_sem=mix_recv,
        device_id=(place, other),
        device_id_type=MESH,
    )

    for a in range(6):
        own_copy(a).start()
    for i in range(2):
        w_own(i).start()
    mix_all[y] = mix_ref[...]
    for ref, filled in ((k_all, rows), (v_all, rows), (tk_all, group * tk_in.shape[0]), (tv_all, group * tv_in.shape[0])):
        if ref.shape[0] > filled:
            ref[filled:, :] = jnp.zeros((ref.shape[0] - filled, ref.shape[1]), ref.dtype)

    pl.semaphore_wait(barrier, len(friends))

    def send_half(h, i):
        for a in range(3 * i, 3 * i + 3):
            for k in range(group - 1, 0, -1):
                in_copy(a, h, k).start()

    send_half(0, 0)
    send_half(0, 1)
    for i in range(2):
        w_copy(i, 0).start()
    for i in range(2):
        w_copy(i, 1).start()
    mix_copy.start()
    for a in range(6):
        own_copy(a).wait()

    gathered = [so_all, co_all]

    def at_copy(i, h, source, way):
        column = pl.ds(pl.multiple_of((source * heads_here + h) * DH, DH), DH)
        return pltpu.make_async_remote_copy(
            src_ref=gathered[i].at[:, column],
            dst_ref=gathered[i].at[:, column],
            send_sem=at_send.at[i, h, source, way],
            recv_sem=at_recv.at[i, h, source],
            device_id=((z + 1 - 2 * way) * TENANTS + t, y),
            device_id_type=MESH,
        )

    def both_ways(i, h, d, act):
        for way in range(2):
            source = z - d if way == 0 else z + d
            onward = z < group - 1 if way == 0 else z > 0
            here = source >= 0 if way == 0 else source < group

            @pl.when(here)
            def _():
                act(at_copy(i, h, source, way), onward)

    def relay(i, h, d):
        def act(copy, onward):
            if d > 0:
                copy.wait_recv()

            @pl.when(onward)
            def _():
                copy.start()

        both_ways(i, h, d, act)

    def settle(i, h, d):
        def act(copy, onward):
            @pl.when(onward)
            def _():
                copy.wait_send()

        both_ways(i, h, d, act)

    def do_head(h, carry):
        here = pl.ds(pl.multiple_of(h * DH, DH), DH)
        column = pl.ds(pl.multiple_of((z * heads_here + h) * DH, DH), DH)
        for i, (qr, kr, vr, count) in enumerate(
            ((q_all, k_all, v_all, my_len), (cq_all, tk_all, tv_all, my_text))
        ):
            for a in range(3 * i, 3 * i + 3):
                for k in range(1, group):
                    in_copy(a, h, k).wait_recv()

            @pl.when(h + 1 < heads_here)
            def _():
                send_half(h + 1, i)

            gathered[i][:, column] = attend_head(qr[:, here], kr[:, here], vr[:, here], count)
            relay(i, h, 0)
            for d in range(1, group):
                back = i - d
                older = h + back // 2

                @pl.when(older >= 0)
                def _():
                    relay(back % 2, older, d)

        return carry

    lax.fori_loop(0, heads_here, do_head, 0)

    for i in range(2):
        w_copy(i, 0).wait_recv()
        w_copy(i, 2).start()
    pieces = 2 * heads_here
    for step in range(pieces, pieces + group - 1):
        for d in range(1, group):
            if step - d < pieces:
                relay((step - d) % 2, (step - d) // 2, d)
    for i in range(2):
        w_own(i).wait()
        w_copy(i, 1).wait_recv()
    for i in range(2):
        w_copy(i, 2).wait_recv()
    mix_copy.wait_recv()

    side = term.shape[1]
    chunks = [(at, min(256, side - at)) for at in range(0, side, 256)]

    def term_copy(j):
        at, n = chunks[j]
        return pltpu.make_async_remote_copy(
            src_ref=term.at[:, pl.ds(at, n)],
            dst_ref=term_in.at[:, pl.ds(at, n)],
            send_sem=term_send.at[j],
            recv_sem=term_recv.at[j],
            device_id=(place, other),
            device_id_type=MESH,
        )

    def project(whose, j):
        at, n = chunks[j]
        start = pl.multiple_of(whose * side + at, 128)
        across_rows = (((1,), (1,)), ((), ()))
        total = lax.dot_general(
            so_all[...], ws_all[pl.ds(start, n), :], across_rows, preferred_element_type=jnp.float32
        )
        first = pl.multiple_of(z * (2 * side) + whose * side + at, 128)
        gates = gate_ref[:, pl.ds(first, n)]
        mine = lax.broadcasted_iota(jnp.int32, gates.shape, 0) == t
        total = jnp.sum(jnp.where(mine, gates, 0.0), axis=0, keepdims=True) * total
        total = total + lax.dot_general(
            co_all[...], wc_all[pl.ds(start, n), :], across_rows, preferred_element_type=jnp.float32
        )
        return total.astype(jnp.bfloat16)

    for j, (at, n) in enumerate(chunks):
        term[:, at : at + n] = project(other, j)
        term_copy(j).start()
    for j, (at, n) in enumerate(chunks):
        term_own[:, at : at + n] = project(y, j)

    source = lax.rem(z, half) * 2 + y

    def out_columns(sender, j):
        at, n = chunks[j]
        return pl.ds(pl.multiple_of(sender * side + at, 128), n)

    def vel_part(j, to):
        at, n = chunks[j]
        return vel.at[pl.ds(pl.multiple_of(to * tiles, 16), tiles), pl.ds(at, n)]

    def out_copy(j, k):
        to = peer(k)
        return pltpu.make_async_remote_copy(
            src_ref=vel_part(j, to),
            dst_ref=out.at[:, out_columns(source, j)],
            send_sem=out_send.at[j, k],
            recv_sem=out_recv.at[source, j],
            device_id=(to * TENANTS + t, y_out),
            device_id_type=MESH,
        )

    def out_own(j):
        return pltpu.make_async_copy(
            vel_part(j, z), out.at[:, out_columns(source, j)], out_local.at[j]
        )

    for j, (at, n) in enumerate(chunks):
        term_copy(j).wait_recv()
        total = term_own[:, at : at + n].astype(jnp.float32)
        total = total + term_in[:, at : at + n].astype(jnp.float32)
        branch = total.astype(jnp.bfloat16).astype(jnp.float32)
        index = lax.broadcasted_iota(jnp.int32, branch.shape, 0)
        branch = jnp.where(index < my_len, branch, 0.0)
        before = jnp.where(index == 0, 0.0, pltpu.roll(branch, 1, 0))
        after = jnp.where(index == rows - 1, 0.0, pltpu.roll(branch, rows - 1, 0))
        mix = mix_all[y_out, :, out_columns(source, j)]
        speed = branch + mix * (before + after - 2.0 * branch)
        vel[:, at : at + n] = jnp.where(index < my_len, speed, 0.0).astype(jnp.bfloat16)
        for k in range(group - 1, 0, -1):
            out_copy(j, k).start()

        @pl.when(y_out == y)
        def _():
            out_own(j).start()

        @pl.when(y_out != y)
        def _():
            out_copy(j, 0).start()

    def drain_head(h, carry):
        for k in range(1, group):
            for a in range(6):
                in_copy(a, h, k).wait_send()
        for i in range(2):
            for d in range(group - 1):
                settle(i, h, d)
        return carry

    lax.fori_loop(0, heads_here, drain_head, 0)
    for i in range(2):
        for hop in range(3):
            w_copy(i, hop).wait_send()
    mix_copy.wait_send()

    for j in range(len(chunks)):
        term_copy(j).wait_send()
        for k in range(1, group):
            out_copy(j, k).wait_send()

        @pl.when(y_out == y)
        def _():
            out_own(j).wait()

        @pl.when(y_out != y)
        def _():
            out_copy(j, 0).wait_send()

    def arrive(sender, carry):
        mine = jnp.logical_and(y_out == y, sender == source)

        @pl.when(jnp.logical_not(mine))
        def _():
            for j in range(len(chunks)):
                pltpu.make_async_remote_copy(
                    src_ref=vel_part(j, 0),
                    dst_ref=out.at[:, out_columns(sender, j)],
                    send_sem=out_send.at[j, 0],
                    recv_sem=out_recv.at[sender, j],
                    device_id=(place, other),
                    device_id_type=MESH,
                ).wait_recv()

        return carry

    lax.fori_loop(0, group, arrive, 0)


def fits(query, text_key, wo_self):
    group = lax.axis_size("req") // TENANTS
    heads = query.shape[1] // DH
    return (
        lax.axis_size("tp") == 2
        and group >= 2
        and group % 2 == 0
        and heads % group == 0
        and query.shape[0] % 16 == 0
        and text_key.shape[0] % 16 == 0
        and wo_self.shape[0] == query.shape[1]
        and wo_self.shape[1] % 64 == 0
    )


def by_heads(
    query,
    key,
    value,
    cross_query,
    text_key,
    text_value,
    wo_self,
    wo_cross,
    attn_gate,
    mix_coef,
    latent,
    tenant_len,
    text_len,
    t_index,
):
    tiles, feat = query.shape
    text_rows = text_key.shape[0]
    blocks = lax.axis_size("req")
    group = blocks // TENANTS
    cols = wo_self.shape[1]
    heads_here = feat // DH // group
    width = heads_here * DH
    rows = tiles * group
    padded = -(-rows // 128) * 128
    texts = -(-text_rows * group // 128) * 128
    place = lax.axis_index("req")
    tenant = place % TENANTS
    slot = place // TENANTS
    side = cols * TENANTS // 2
    chunks = -(-side // 256)
    mix = mix_coef.reshape(1, -1)
    bf = jnp.bfloat16
    dma = pltpu.SemaphoreType.DMA
    any_spec = pl.BlockSpec(memory_space=pltpu.HBM)
    smem = pl.BlockSpec(memory_space=pltpu.SMEM)
    vmem = pl.BlockSpec(memory_space=pltpu.VMEM)
    flops = 4 * rows * width * (padded + texts) + 4 * rows * feat * TENANTS * cols
    velocity = pl.pallas_call(
        functools.partial(fused_kernel, group),
        out_shape=jax.ShapeDtypeStruct((tiles, blocks // 2 * cols), bf),
        in_specs=[smem, smem] + [any_spec] * 8 + [vmem, vmem],
        out_specs=any_spec,
        scratch_shapes=[
            pltpu.VMEM((rows, width), bf),
            pltpu.VMEM((padded, width), bf),
            pltpu.VMEM((padded, width), bf),
            pltpu.VMEM((rows, width), bf),
            pltpu.VMEM((texts, width), bf),
            pltpu.VMEM((texts, width), bf),
            pltpu.VMEM((rows, feat), bf),
            pltpu.VMEM((rows, feat), bf),
            pltpu.VMEM((TENANTS * cols, feat), bf),
            pltpu.VMEM((TENANTS * cols, feat), bf),
            pltpu.VMEM((2, 1, blocks // 2 * cols), jnp.float32),
            pltpu.VMEM((rows, side), bf),
            pltpu.VMEM((rows, side), bf),
            pltpu.VMEM((rows, side), bf),
            pltpu.VMEM((rows, side), bf),
            dma((6, heads_here, group - 1)),
            dma((6, heads_here, group - 1)),
            dma((6,)),
            dma((2, 3)),
            dma((2, 3)),
            dma((2,)),
            dma,
            dma,
            dma((2, heads_here, group, 2)),
            dma((2, heads_here, group)),
            dma((chunks,)),
            dma((chunks,)),
            dma((chunks, group)),
            dma((group, chunks)),
            dma((chunks,)),
        ],
        compiler_params=pltpu.CompilerParams(
            collective_id=0, has_side_effects=True, vmem_limit_bytes=60 * 1024 * 1024
        ),
        cost_estimate=pl.CostEstimate(
            flops=flops, bytes_accessed=16 * feat * cols, transcendentals=rows * heads_here * (padded + texts)
        ),
        name="attend_project",
    )(
        tenant_len,
        text_len,
        query,
        key,
        value,
        cross_query,
        text_key,
        text_value,
        wo_self.T,
        wo_cross.T,
        attn_gate,
        mix,
    )
    step = jnp.sum(jnp.where(jnp.arange(TENANTS) == tenant, t_index, 0))
    frac = 1.0 - step.astype(jnp.float32) / STEPS
    sigma = 5.0 * frac / (1.0 + 4.0 * frac)
    return (velocity, latent.astype(jnp.float32) + sigma * velocity.astype(jnp.float32))


def either(*arrays):
    if fits(arrays[0], arrays[4], arrays[6]):
        return by_heads(*arrays)
    return shards(*arrays)


def solution(mesh):
    placed = (
        P("req", "tp"),
        P("req", "tp"),
        P("req", "tp"),
        P("req", "tp"),
        P("req", "tp"),
        P("req", "tp"),
        P("tp", "req"),
        P("tp", "req"),
        P(),
        P("tp"),
        P("req", "tp"),
        P(),
        P(),
        P(),
    )
    return jax.shard_map(
        either,
        mesh=mesh,
        in_specs=placed,
        out_specs=(P("req", "tp"), P("req", "tp")),
        check_vma=False,
    )
```

```python
import functools

import jax
import jax.numpy as jnp
from jax import lax
from jax.experimental import pallas as pl
from jax.experimental.pallas import tpu as pltpu
from jax.sharding import PartitionSpec as P

DH = 128
TENANTS = 4
STEPS = 50


def passed_along(block, axis, distance):
    devices = range(lax.axis_size(axis))
    route = [((i - distance) % len(devices), i) for i in devices]
    return lax.ppermute(block, axis, route)


def shifted(block, axis, distance):
    devices = range(lax.axis_size(axis))
    route = [(i - distance, i) for i in devices if i - distance in devices]
    return lax.ppermute(block, axis, route)


def attend_block(state, q_heads, k_block, v_block, valid):
    top, denom, accum = state
    heads = q_heads.shape[1]
    k_heads = k_block.reshape(k_block.shape[0], heads, DH)
    v_heads = v_block.reshape(v_block.shape[0], heads, DH)
    scores = jnp.einsum("qhd,khd->hqk", q_heads, k_heads, preferred_element_type=jnp.float32) * (
        1.0 / DH**0.5
    )
    scores = jnp.where(valid[None, None, :], scores, -1e30)
    new_top = jnp.maximum(top, jnp.max(scores, axis=-1))
    weights = jnp.where(valid[None, None, :], jnp.exp(scores - new_top[..., None]), 0.0)
    factor = jnp.exp(top - new_top)
    denom = denom * factor + jnp.sum(weights, axis=-1)
    mixed = jnp.einsum(
        "hqk,khd->hqd", weights.astype(jnp.bfloat16), v_heads, preferred_element_type=jnp.float32
    )
    return (new_top, denom, accum * factor[..., None] + mixed)


def finish(state, tiles, feat):
    top, denom, accum = state
    out = accum / denom[..., None]
    return out.transpose(1, 0, 2).reshape(tiles, feat).astype(jnp.bfloat16)


def shards(
    query,
    key,
    value,
    cross_query,
    text_key,
    text_value,
    wo_self,
    wo_cross,
    attn_gate,
    mix_coef,
    latent,
    tenant_len,
    text_len,
    t_index,
):
    tiles, feat = query.shape
    text_rows = text_key.shape[0]
    heads = feat // DH
    group = lax.axis_size("req") // TENANTS
    place = lax.axis_index("req")
    tenant = place % TENANTS
    slot = place // TENANTS
    picker = jnp.arange(TENANTS) == tenant
    my_len = jnp.sum(jnp.where(picker, tenant_len, 0))
    my_text = jnp.sum(jnp.where(picker, text_len, 0))
    my_step = jnp.sum(jnp.where(picker, t_index, 0))
    gate_row = jnp.sum(jnp.where(picker[:, None], attn_gate, 0.0), axis=0)
    q_heads = query.reshape(tiles, heads, DH)
    cq_heads = cross_query.reshape(tiles, heads, DH)
    row_ids = jnp.arange(tiles, dtype=jnp.int32)

    def absorb(held, blocks, root):
        state, text_keys, text_values = held
        k_block, v_block, tk_block, tv_block = blocks
        valid = root * tiles + row_ids < my_len
        state = attend_block(state, q_heads, k_block, v_block, valid)
        text_keys = lax.dynamic_update_slice_in_dim(text_keys, tk_block, root * text_rows, 0)
        text_values = lax.dynamic_update_slice_in_dim(text_values, tv_block, root * text_rows, 0)
        return (state, text_keys, text_values)

    def fresh(count):
        return (
            jnp.full((heads, count), -1e30, jnp.float32),
            jnp.zeros((heads, count), jnp.float32),
            jnp.zeros((heads, count, DH), jnp.float32),
        )

    all_text = group * text_rows
    empty_text = jnp.zeros((all_text, feat), text_key.dtype)
    start_blocks = (key, value, text_key, text_value)
    held = absorb((fresh(tiles), empty_text, empty_text), start_blocks, slot)

    def turn_cycle(j, carry):
        blocks, kept = carry
        blocks = passed_along((blocks[0], blocks[1], blocks[2], blocks[3]), "req", TENANTS)
        return (blocks, absorb(kept, blocks, (slot - j) % group))

    _, held = lax.fori_loop(1, group, turn_cycle, (start_blocks, held))
    self_state, text_keys, text_values = held
    self_out = finish(self_state, tiles, feat)
    text_valid = jnp.arange(all_text, dtype=jnp.int32) < my_text
    cross_state = attend_block(fresh(tiles), cq_heads, text_keys, text_values, text_valid)
    cross_out = finish(cross_state, tiles, feat)
    self_cols = lax.all_gather(wo_self, "req", axis=1, tiled=True)
    cross_cols = lax.all_gather(wo_cross, "req", axis=1, tiled=True)
    block = gate_row[None, :] * jnp.dot(self_out, self_cols, preferred_element_type=jnp.float32)
    block = block + jnp.dot(cross_out, cross_cols, preferred_element_type=jnp.float32)
    summed = lax.psum_scatter(block.astype(jnp.bfloat16), "tp", scatter_dimension=1, tiled=True)
    valid_rows = slot * tiles + row_ids < my_len
    branch = jnp.where(valid_rows[:, None], summed, jnp.zeros((), jnp.bfloat16))
    before = shifted(branch[-1:], "req", TENANTS)
    after = shifted(branch[:1], "req", -TENANTS)
    extended = jnp.concatenate([before, branch, after], axis=0).astype(jnp.float32)
    branch32 = branch.astype(jnp.float32)
    vel = branch32 + mix_coef[None, :] * (extended[:-2] + extended[2:] - 2.0 * branch32)
    vel = jnp.where(valid_rows[:, None], vel, 0.0)
    frac = 1.0 - my_step.astype(jnp.float32) / STEPS
    sigma = 5.0 * frac / (1.0 + 4.0 * frac)
    updated = latent.astype(jnp.float32) + sigma * vel
    return (vel.astype(jnp.bfloat16), updated)


MESH = pl.DeviceIdType.MESH


def attend_head(q, k, v, count):
    scores = lax.dot_general(
        q, k, (((1,), (1,)), ((), ())), preferred_element_type=jnp.float32
    ) * (1.0 / DH**0.5)
    valid = lax.broadcasted_iota(jnp.int32, scores.shape, 1) < count
    scores = jnp.where(valid, scores, -1e30)
    top = jnp.max(scores, axis=-1, keepdims=True)
    weights = jnp.where(valid, jnp.exp(scores - top), 0.0)
    denom = jnp.sum(weights, axis=-1, keepdims=True)
    mixed = jnp.dot(weights.astype(jnp.bfloat16), v, preferred_element_type=jnp.float32)
    return (mixed / denom).astype(jnp.bfloat16)


def fused_kernel(
    group,
    len_ref,
    text_ref,
    step_ref,
    q_in,
    k_in,
    v_in,
    cq_in,
    tk_in,
    tv_in,
    ws_in,
    wc_in,
    gate_ref,
    mix_ref,
    out,
    sigma_ref,
    q_all,
    k_all,
    v_all,
    cq_all,
    tk_all,
    tv_all,
    so_all,
    co_all,
    ws_all,
    wc_all,
    mix_all,
    acc,
    term,
    term_own,
    term_in,
    vel,
    in_send,
    in_recv,
    in_local,
    w_send,
    w_recv,
    w_local,
    mix_local,
    mix_send,
    mix_recv,
    at_send,
    at_recv,
    term_send,
    term_recv,
    out_send,
    out_recv,
    out_local,
):
    place = lax.axis_index("req")
    y = lax.axis_index("tp")
    t = lax.rem(place, TENANTS)
    z = place // TENANTS
    half = group // 2
    tiles = q_in.shape[0]
    rows = tiles * group
    heads_here = q_in.shape[1] // (DH * group)
    sibling = t + 1 - 2 * lax.rem(t, 2)
    across = lax.rem(t + 2, TENANTS)
    other = 1 - y
    y_out = z // half
    my_len = len_ref[t]
    my_text = text_ref[t]

    def peer(k):
        return lax.rem(z + k, group)

    barrier = pltpu.get_barrier_semaphore()
    friends = [(z * TENANTS + sibling, y), (z * TENANTS + across, y), (place, other)]
    for k in range(1, group):
        friends += [(peer(k) * TENANTS + t, y), (peer(k) * TENANTS + t, other)]
    for friend in friends:
        pl.semaphore_signal(barrier, inc=1, device_id=friend, device_id_type=MESH)

    moved = [
        (q_in, q_all),
        (k_in, k_all),
        (v_in, v_all),
        (cq_in, cq_all),
        (tk_in, tk_all),
        (tv_in, tv_all),
    ]

    def own_copy(a):
        src, dst = moved[a]
        n = src.shape[0]
        width = heads_here * DH
        return pltpu.make_async_copy(
            src.at[:, pl.ds(pl.multiple_of(z * width, DH), width)],
            dst.at[pl.ds(pl.multiple_of(z * n, 16), n), :],
            in_local.at[a],
        )

    def in_copy(a, h, k):
        src, dst = moved[a]
        n = src.shape[0]
        to = peer(k)
        return pltpu.make_async_remote_copy(
            src_ref=src.at[:, pl.ds(pl.multiple_of((to * heads_here + h) * DH, DH), DH)],
            dst_ref=dst.at[
                pl.ds(pl.multiple_of(z * n, 16), n), pl.ds(pl.multiple_of(h * DH, DH), DH)
            ],
            send_sem=in_send.at[a, h, k - 1],
            recv_sem=in_recv.at[a, h, k - 1],
            device_id=(to * TENANTS + t, y),
            device_id_type=MESH,
        )

    weights = [(ws_in, ws_all), (wc_in, wc_all)]

    cols = ws_in.shape[0]

    def w_rows(block):
        return pl.ds(pl.multiple_of(block * cols, 16), cols)

    def w_own(i):
        src, dst = weights[i]
        return pltpu.make_async_copy(src, dst.at[w_rows(t), :], w_local.at[i])

    def w_copy(i, hop):
        src, dst = weights[i]
        if hop == 2:
            src, block = dst.at[w_rows(across), :], across
        else:
            block = t
        target = across if hop == 0 else sibling
        return pltpu.make_async_remote_copy(
            src_ref=src,
            dst_ref=dst.at[w_rows(block), :],
            send_sem=w_send.at[i, hop],
            recv_sem=w_recv.at[i, hop],
            device_id=(z * TENANTS + target, y),
            device_id_type=MESH,
        )

    mix_copy = pltpu.make_async_remote_copy(
        src_ref=mix_all.at[y],
        dst_ref=mix_all.at[y],
        send_sem=mix_send,
        recv_sem=mix_recv,
        device_id=(place, other),
        device_id_type=MESH,
    )

    for a in range(6):
        own_copy(a).start()
    for i in range(2):
        w_own(i).start()
    mix_own = pltpu.make_async_copy(mix_ref, mix_all.at[y], mix_local)
    mix_own.start()
    frac = 1.0 - jnp.full(sigma_ref.shape, step_ref[t], jnp.int32).astype(jnp.float32) / STEPS
    sigma_ref[...] = 5.0 * frac / (1.0 + 4.0 * frac)
    for ref, filled in ((k_all, rows), (v_all, rows), (tk_all, group * tk_in.shape[0]), (tv_all, group * tv_in.shape[0])):
        if ref.shape[0] > filled:
            ref[filled:, :] = jnp.zeros((ref.shape[0] - filled, ref.shape[1]), ref.dtype)

    pl.semaphore_wait(barrier, len(friends))

    def send_half(h, i):
        for a in range(3 * i, 3 * i + 3):
            for k in range(group - 1, 0, -1):
                in_copy(a, h, k).start()

    send_half(0, 0)
    send_half(0, 1)
    for i in range(2):
        w_copy(i, 0).start()
    for i in range(2):
        w_copy(i, 1).start()
    mix_own.wait()
    mix_copy.start()
    for a in range(6):
        own_copy(a).wait()

    gathered = [so_all, co_all]

    def at_copy(i, h, source, way):
        column = pl.ds(pl.multiple_of((source * heads_here + h) * DH, DH), DH)
        return pltpu.make_async_remote_copy(
            src_ref=gathered[i].at[:, column],
            dst_ref=gathered[i].at[:, column],
            send_sem=at_send.at[i, h, source, way],
            recv_sem=at_recv.at[i, h, source],
            device_id=((z + 1 - 2 * way) * TENANTS + t, y),
            device_id_type=MESH,
        )

    def both_ways(i, h, d, act):
        for way in range(2):
            source = z - d if way == 0 else z + d
            onward = z < group - 1 if way == 0 else z > 0
            here = source >= 0 if way == 0 else source < group

            @pl.when(here)
            def _():
                act(at_copy(i, h, source, way), onward)

    def relay(i, h, d):
        def act(copy, onward):
            if d > 0:
                copy.wait_recv()

            @pl.when(onward)
            def _():
                copy.start()

        both_ways(i, h, d, act)

    def settle(i, h, d):
        def act(copy, onward):
            @pl.when(onward)
            def _():
                copy.wait_send()

        both_ways(i, h, d, act)

    def do_head(h, carry):
        here = pl.ds(pl.multiple_of(h * DH, DH), DH)
        column = pl.ds(pl.multiple_of((z * heads_here + h) * DH, DH), DH)
        for i, (qr, kr, vr, count) in enumerate(
            ((q_all, k_all, v_all, my_len), (cq_all, tk_all, tv_all, my_text))
        ):
            for a in range(3 * i, 3 * i + 3):
                for k in range(1, group):
                    in_copy(a, h, k).wait_recv()

            @pl.when(h == heads_here - 1)
            def _():
                w_copy(i, 0).wait_recv()
                w_copy(i, 2).start()

            @pl.when(h + 1 < heads_here)
            def _():
                send_half(h + 1, i)

            gathered[i][:, column] = attend_head(qr[:, here], kr[:, here], vr[:, here], count)
            relay(i, h, 0)
            for d in range(1, group):
                back = i - d
                older = h + back // 2

                @pl.when(older >= 0)
                def _():
                    relay(back % 2, older, d)

        return carry

    lax.fori_loop(0, heads_here, do_head, 0)

    side = term.shape[1]
    lead = side % 256
    chunks = [(0, lead)] if lead else []
    chunks += [(at, 256) for at in range(lead, side, 256)]

    def term_copy(j):
        at, n = chunks[j]
        return pltpu.make_async_remote_copy(
            src_ref=term.at[:, pl.ds(at, n)],
            dst_ref=term_in.at[:, pl.ds(at, n)],
            send_sem=term_send.at[j],
            recv_sem=term_recv.at[j],
            device_id=(place, other),
            device_id_type=MESH,
        )

    def part(h, whose, j):
        at, n = chunks[j]
        places = [slice((s * heads_here + h) * DH, (s * heads_here + h + 1) * DH) for s in range(group)]
        start = pl.multiple_of(whose * side + at, 128)
        first = pl.multiple_of(z * (2 * side) + whose * side + at, 128)
        gates = gate_ref[:, pl.ds(first, n)]
        mine = lax.broadcasted_iota(jnp.int32, gates.shape, 0) == t
        gates = jnp.sum(jnp.where(mine, gates, 0.0), axis=0, keepdims=True)

        def product(left, right):
            return lax.dot_general(
                jnp.concatenate([left[:, p] for p in places], axis=1),
                jnp.concatenate([right[pl.ds(start, n), p] for p in places], axis=1),
                (((1,), (1,)), ((), ())),
                preferred_element_type=jnp.float32,
            )

        return gates * product(so_all, ws_all) + product(co_all, wc_all)

    def sums(whose, j):
        at, n = chunks[j]
        return (slice(None), pl.ds(pl.multiple_of(whose * side + at, 128), n))

    def add_head(h):
        for whose in (other, y):
            for j in range(len(chunks)):
                total = part(h, whose, j)
                if h > 0:
                    total = acc[sums(whose, j)] + total
                acc[sums(whose, j)] = total

    def last_head(whose, j):
        total = part(heads_here - 1, whose, j)
        if heads_here > 1:
            total = acc[sums(whose, j)] + total
        return total.astype(jnp.bfloat16)

    pieces = 2 * heads_here
    added = 0
    for step in range(pieces, pieces + group - 1):
        for d in range(1, group):
            if step - d < pieces:
                relay((step - d) % 2, (step - d) // 2, d)
        if step == pieces:
            for i in range(2):
                w_own(i).wait()
                w_copy(i, 1).wait_recv()
            for i in range(2):
                w_copy(i, 2).wait_recv()
        if added < heads_here - 1 and 2 * added + group <= step:
            add_head(added)
            added += 1
    mix_copy.wait_recv()
    while added < heads_here - 1:
        add_head(added)
        added += 1

    for j, (at, n) in enumerate(chunks):
        term[:, at : at + n] = last_head(other, j)
        term_copy(j).start()
    for j, (at, n) in enumerate(chunks):
        term_own[:, at : at + n] = last_head(y, j)

    source = lax.rem(z, half) * 2 + y

    def out_columns(sender, j):
        at, n = chunks[j]
        return pl.ds(pl.multiple_of(sender * side + at, 128), n)

    def vel_part(j, to):
        at, n = chunks[j]
        return vel.at[pl.ds(pl.multiple_of(to * tiles, 16), tiles), pl.ds(at, n)]

    def out_copy(j, k):
        to = peer(k)
        return pltpu.make_async_remote_copy(
            src_ref=vel_part(j, to),
            dst_ref=out.at[:, out_columns(source, j)],
            send_sem=out_send.at[j, k],
            recv_sem=out_recv.at[source, j],
            device_id=(to * TENANTS + t, y_out),
            device_id_type=MESH,
        )

    def out_own(j):
        return pltpu.make_async_copy(
            vel_part(j, z), out.at[:, out_columns(source, j)], out_local.at[j]
        )

    for j, (at, n) in enumerate(chunks):
        term_copy(j).wait_recv()
        total = term_own[:, at : at + n].astype(jnp.float32)
        total = total + term_in[:, at : at + n].astype(jnp.float32)
        branch = total.astype(jnp.bfloat16).astype(jnp.float32)
        index = lax.broadcasted_iota(jnp.int32, branch.shape, 0)
        branch = jnp.where(index < my_len, branch, 0.0)
        before = jnp.where(index == 0, 0.0, pltpu.roll(branch, 1, 0))
        after = jnp.where(index == rows - 1, 0.0, pltpu.roll(branch, rows - 1, 0))
        line = (source * side + at) // DH
        mix = jnp.concatenate([mix_all[y_out, pl.ds(line + m, 1), :] for m in range(n // DH)], axis=1)
        speed = branch + mix * (before + after - 2.0 * branch)
        vel[:, at : at + n] = jnp.where(index < my_len, speed, 0.0).astype(jnp.bfloat16)
        for k in range(group - 1, 0, -1):
            out_copy(j, k).start()

        @pl.when(y_out == y)
        def _():
            out_own(j).start()

        @pl.when(y_out != y)
        def _():
            out_copy(j, 0).start()

    def drain_head(h, carry):
        for k in range(1, group):
            for a in range(6):
                in_copy(a, h, k).wait_send()
        for i in range(2):
            for d in range(group - 1):
                settle(i, h, d)
        return carry

    lax.fori_loop(0, heads_here, drain_head, 0)
    for i in range(2):
        for hop in range(3):
            w_copy(i, hop).wait_send()
    mix_copy.wait_send()

    for j in range(len(chunks)):
        term_copy(j).wait_send()
        for k in range(1, group):
            out_copy(j, k).wait_send()

        @pl.when(y_out == y)
        def _():
            out_own(j).wait()

        @pl.when(y_out != y)
        def _():
            out_copy(j, 0).wait_send()

    def arrive(sender, carry):
        mine = jnp.logical_and(y_out == y, sender == source)

        @pl.when(jnp.logical_not(mine))
        def _():
            for j in range(len(chunks)):
                pltpu.make_async_remote_copy(
                    src_ref=vel_part(j, 0),
                    dst_ref=out.at[:, out_columns(sender, j)],
                    send_sem=out_send.at[j, 0],
                    recv_sem=out_recv.at[sender, j],
                    device_id=(place, other),
                    device_id_type=MESH,
                ).wait_recv()

        return carry

    lax.fori_loop(0, group, arrive, 0)


def fits(query, text_key, wo_self):
    group = lax.axis_size("req") // TENANTS
    heads = query.shape[1] // DH
    return (
        lax.axis_size("tp") == 2
        and group >= 2
        and group % 2 == 0
        and heads % group == 0
        and query.shape[0] % 16 == 0
        and text_key.shape[0] % 16 == 0
        and wo_self.shape[0] == query.shape[1]
        and wo_self.shape[1] % 64 == 0
    )


def by_heads(
    query,
    key,
    value,
    cross_query,
    text_key,
    text_value,
    wo_self,
    wo_cross,
    attn_gate,
    mix_coef,
    latent,
    tenant_len,
    text_len,
    t_index,
):
    tiles, feat = query.shape
    text_rows = text_key.shape[0]
    blocks = lax.axis_size("req")
    group = blocks // TENANTS
    cols = wo_self.shape[1]
    heads_here = feat // DH // group
    width = heads_here * DH
    rows = tiles * group
    padded = -(-rows // 128) * 128
    texts = -(-text_rows * group // 128) * 128
    side = cols * TENANTS // 2
    chunks = -(-side // 256)
    mix = mix_coef.reshape(-1, DH)
    bf = jnp.bfloat16
    dma = pltpu.SemaphoreType.DMA
    any_spec = pl.BlockSpec(memory_space=pltpu.HBM)
    smem = pl.BlockSpec(memory_space=pltpu.SMEM)
    vmem = pl.BlockSpec(memory_space=pltpu.VMEM)
    flops = 4 * rows * width * (padded + texts) + 4 * rows * feat * TENANTS * cols
    velocity, sigma = pl.pallas_call(
        functools.partial(fused_kernel, group),
        out_shape=(
            jax.ShapeDtypeStruct((tiles, blocks // 2 * cols), bf),
            jax.ShapeDtypeStruct((1, 128), jnp.float32),
        ),
        in_specs=[smem] * 3 + [any_spec] * 8 + [vmem, any_spec],
        out_specs=(any_spec, vmem),
        scratch_shapes=[
            pltpu.VMEM((rows, width), bf),
            pltpu.VMEM((padded, width), bf),
            pltpu.VMEM((padded, width), bf),
            pltpu.VMEM((rows, width), bf),
            pltpu.VMEM((texts, width), bf),
            pltpu.VMEM((texts, width), bf),
            pltpu.VMEM((rows, feat), bf),
            pltpu.VMEM((rows, feat), bf),
            pltpu.VMEM((TENANTS * cols, feat), bf),
            pltpu.VMEM((TENANTS * cols, feat), bf),
            pltpu.VMEM((2, blocks // 2 * cols // DH, DH), jnp.float32),
            pltpu.VMEM((rows, 2 * side), jnp.float32),
            pltpu.VMEM((rows, side), bf),
            pltpu.VMEM((rows, side), bf),
            pltpu.VMEM((rows, side), bf),
            pltpu.VMEM((rows, side), bf),
            dma((6, heads_here, group - 1)),
            dma((6, heads_here, group - 1)),
            dma((6,)),
            dma((2, 3)),
            dma((2, 3)),
            dma((2,)),
            dma,
            dma,
            dma,
            dma((2, heads_here, group, 2)),
            dma((2, heads_here, group)),
            dma((chunks,)),
            dma((chunks,)),
            dma((chunks, group)),
            dma((group, chunks)),
            dma((chunks,)),
        ],
        compiler_params=pltpu.CompilerParams(
            collective_id=0, has_side_effects=True, vmem_limit_bytes=60 * 1024 * 1024
        ),
        cost_estimate=pl.CostEstimate(
            flops=flops, bytes_accessed=16 * feat * cols, transcendentals=rows * heads_here * (padded + texts)
        ),
        name="attend_project",
    )(
        tenant_len,
        text_len,
        t_index,
        query,
        key,
        value,
        cross_query,
        text_key,
        text_value,
        wo_self.T,
        wo_cross.T,
        attn_gate,
        mix,
    )
    return (velocity, latent.astype(jnp.float32) + sigma[0, 0] * velocity.astype(jnp.float32))


def either(*arrays):
    if fits(arrays[0], arrays[4], arrays[6]):
        return by_heads(*arrays)
    return shards(*arrays)


def solution(mesh):
    placed = (
        P("req", "tp"),
        P("req", "tp"),
        P("req", "tp"),
        P("req", "tp"),
        P("req", "tp"),
        P("req", "tp"),
        P("tp", "req"),
        P("tp", "req"),
        P(),
        P("tp"),
        P("req", "tp"),
        P(),
        P(),
        P(),
    )
    return jax.shard_map(
        either,
        mesh=mesh,
        in_specs=placed,
        out_specs=(P("req", "tp"), P("req", "tp")),
        check_vma=False,
    )
```

```python
import functools

import jax
import jax.numpy as jnp
from jax import lax
from jax.experimental import pallas as pl
from jax.experimental.pallas import tpu as pltpu
from jax.sharding import PartitionSpec as P

DH = 128
TENANTS = 4
STEPS = 50


def passed_along(block, axis, distance):
    devices = range(lax.axis_size(axis))
    route = [((i - distance) % len(devices), i) for i in devices]
    return lax.ppermute(block, axis, route)


def shifted(block, axis, distance):
    devices = range(lax.axis_size(axis))
    route = [(i - distance, i) for i in devices if i - distance in devices]
    return lax.ppermute(block, axis, route)


def attend_block(state, q_heads, k_block, v_block, valid):
    top, denom, accum = state
    heads = q_heads.shape[1]
    k_heads = k_block.reshape(k_block.shape[0], heads, DH)
    v_heads = v_block.reshape(v_block.shape[0], heads, DH)
    scores = jnp.einsum("qhd,khd->hqk", q_heads, k_heads, preferred_element_type=jnp.float32) * (
        1.0 / DH**0.5
    )
    scores = jnp.where(valid[None, None, :], scores, -1e30)
    new_top = jnp.maximum(top, jnp.max(scores, axis=-1))
    weights = jnp.where(valid[None, None, :], jnp.exp(scores - new_top[..., None]), 0.0)
    factor = jnp.exp(top - new_top)
    denom = denom * factor + jnp.sum(weights, axis=-1)
    mixed = jnp.einsum(
        "hqk,khd->hqd", weights.astype(jnp.bfloat16), v_heads, preferred_element_type=jnp.float32
    )
    return (new_top, denom, accum * factor[..., None] + mixed)


def finish(state, tiles, feat):
    top, denom, accum = state
    out = accum / denom[..., None]
    return out.transpose(1, 0, 2).reshape(tiles, feat).astype(jnp.bfloat16)


def shards(
    query,
    key,
    value,
    cross_query,
    text_key,
    text_value,
    wo_self,
    wo_cross,
    attn_gate,
    mix_coef,
    latent,
    tenant_len,
    text_len,
    t_index,
):
    tiles, feat = query.shape
    text_rows = text_key.shape[0]
    heads = feat // DH
    group = lax.axis_size("req") // TENANTS
    place = lax.axis_index("req")
    tenant = place % TENANTS
    slot = place // TENANTS
    picker = jnp.arange(TENANTS) == tenant
    my_len = jnp.sum(jnp.where(picker, tenant_len, 0))
    my_text = jnp.sum(jnp.where(picker, text_len, 0))
    my_step = jnp.sum(jnp.where(picker, t_index, 0))
    gate_row = jnp.sum(jnp.where(picker[:, None], attn_gate, 0.0), axis=0)
    q_heads = query.reshape(tiles, heads, DH)
    cq_heads = cross_query.reshape(tiles, heads, DH)
    row_ids = jnp.arange(tiles, dtype=jnp.int32)

    def absorb(held, blocks, root):
        state, text_keys, text_values = held
        k_block, v_block, tk_block, tv_block = blocks
        valid = root * tiles + row_ids < my_len
        state = attend_block(state, q_heads, k_block, v_block, valid)
        text_keys = lax.dynamic_update_slice_in_dim(text_keys, tk_block, root * text_rows, 0)
        text_values = lax.dynamic_update_slice_in_dim(text_values, tv_block, root * text_rows, 0)
        return (state, text_keys, text_values)

    def fresh(count):
        return (
            jnp.full((heads, count), -1e30, jnp.float32),
            jnp.zeros((heads, count), jnp.float32),
            jnp.zeros((heads, count, DH), jnp.float32),
        )

    all_text = group * text_rows
    empty_text = jnp.zeros((all_text, feat), text_key.dtype)
    start_blocks = (key, value, text_key, text_value)
    held = absorb((fresh(tiles), empty_text, empty_text), start_blocks, slot)

    def turn_cycle(j, carry):
        blocks, kept = carry
        blocks = passed_along((blocks[0], blocks[1], blocks[2], blocks[3]), "req", TENANTS)
        return (blocks, absorb(kept, blocks, (slot - j) % group))

    _, held = lax.fori_loop(1, group, turn_cycle, (start_blocks, held))
    self_state, text_keys, text_values = held
    self_out = finish(self_state, tiles, feat)
    text_valid = jnp.arange(all_text, dtype=jnp.int32) < my_text
    cross_state = attend_block(fresh(tiles), cq_heads, text_keys, text_values, text_valid)
    cross_out = finish(cross_state, tiles, feat)
    self_cols = lax.all_gather(wo_self, "req", axis=1, tiled=True)
    cross_cols = lax.all_gather(wo_cross, "req", axis=1, tiled=True)
    block = gate_row[None, :] * jnp.dot(self_out, self_cols, preferred_element_type=jnp.float32)
    block = block + jnp.dot(cross_out, cross_cols, preferred_element_type=jnp.float32)
    summed = lax.psum_scatter(block.astype(jnp.bfloat16), "tp", scatter_dimension=1, tiled=True)
    valid_rows = slot * tiles + row_ids < my_len
    branch = jnp.where(valid_rows[:, None], summed, jnp.zeros((), jnp.bfloat16))
    before = shifted(branch[-1:], "req", TENANTS)
    after = shifted(branch[:1], "req", -TENANTS)
    extended = jnp.concatenate([before, branch, after], axis=0).astype(jnp.float32)
    branch32 = branch.astype(jnp.float32)
    vel = branch32 + mix_coef[None, :] * (extended[:-2] + extended[2:] - 2.0 * branch32)
    vel = jnp.where(valid_rows[:, None], vel, 0.0)
    frac = 1.0 - my_step.astype(jnp.float32) / STEPS
    sigma = 5.0 * frac / (1.0 + 4.0 * frac)
    updated = latent.astype(jnp.float32) + sigma * vel
    return (vel.astype(jnp.bfloat16), updated)


MESH = pl.DeviceIdType.MESH


def attend_head(q, k, v, count):
    scores = lax.dot_general(
        q, k, (((1,), (1,)), ((), ())), preferred_element_type=jnp.float32
    ) * (1.0 / DH**0.5)
    valid = lax.broadcasted_iota(jnp.int32, scores.shape, 1) < count
    scores = jnp.where(valid, scores, -1e30)
    top = jnp.max(scores, axis=-1, keepdims=True)
    weights = jnp.where(valid, jnp.exp(scores - top), 0.0)
    denom = jnp.sum(weights, axis=-1, keepdims=True)
    mixed = jnp.dot(weights.astype(jnp.bfloat16), v, preferred_element_type=jnp.float32)
    return (mixed / denom).astype(jnp.bfloat16)


def fused_kernel(
    group,
    len_ref,
    text_ref,
    step_ref,
    q_in,
    k_in,
    v_in,
    cq_in,
    tk_in,
    tv_in,
    ws_in,
    wc_in,
    gate_ref,
    mix_ref,
    out,
    sigma_ref,
    q_all,
    k_all,
    v_all,
    cq_all,
    tk_all,
    tv_all,
    so_all,
    co_all,
    ws_all,
    wc_all,
    mix_all,
    term,
    term_own,
    term_in,
    vel,
    in_send,
    in_recv,
    in_local,
    w_send,
    w_recv,
    w_local,
    mix_local,
    mix_send,
    mix_recv,
    at_send,
    at_recv,
    term_send,
    term_recv,
    out_send,
    out_recv,
    out_local,
):
    place = lax.axis_index("req")
    y = lax.axis_index("tp")
    t = lax.rem(place, TENANTS)
    z = place // TENANTS
    half = group // 2
    tiles = q_in.shape[0]
    rows = tiles * group
    heads_here = q_in.shape[1] // (DH * group)
    sibling = t + 1 - 2 * lax.rem(t, 2)
    across = lax.rem(t + 2, TENANTS)
    other = 1 - y
    y_out = z // half
    my_len = len_ref[t]
    my_text = text_ref[t]

    def peer(k):
        return lax.rem(z + k, group)

    barrier = pltpu.get_barrier_semaphore()
    friends = [(z * TENANTS + sibling, y), (z * TENANTS + across, y), (place, other)]
    for k in range(1, group):
        friends += [(peer(k) * TENANTS + t, y), (peer(k) * TENANTS + t, other)]
    for friend in friends:
        pl.semaphore_signal(barrier, inc=1, device_id=friend, device_id_type=MESH)

    moved = [
        (q_in, q_all),
        (k_in, k_all),
        (v_in, v_all),
        (cq_in, cq_all),
        (tk_in, tk_all),
        (tv_in, tv_all),
    ]

    def own_copy(a):
        src, dst = moved[a]
        n = src.shape[0]
        width = heads_here * DH
        return pltpu.make_async_copy(
            src.at[:, pl.ds(pl.multiple_of(z * width, DH), width)],
            dst.at[pl.ds(pl.multiple_of(z * n, 16), n), :],
            in_local.at[a],
        )

    def in_copy(a, h, k):
        src, dst = moved[a]
        n = src.shape[0]
        to = peer(k)
        return pltpu.make_async_remote_copy(
            src_ref=src.at[:, pl.ds(pl.multiple_of((to * heads_here + h) * DH, DH), DH)],
            dst_ref=dst.at[
                pl.ds(pl.multiple_of(z * n, 16), n), pl.ds(pl.multiple_of(h * DH, DH), DH)
            ],
            send_sem=in_send.at[a, h, k - 1],
            recv_sem=in_recv.at[a, h, k - 1],
            device_id=(to * TENANTS + t, y),
            device_id_type=MESH,
        )

    weights = [(ws_in, ws_all), (wc_in, wc_all)]

    cols = ws_in.shape[0]

    def w_rows(block):
        return pl.ds(pl.multiple_of(block * cols, 16), cols)

    def w_own(i):
        src, dst = weights[i]
        return pltpu.make_async_copy(src, dst.at[w_rows(t), :], w_local.at[i])

    def w_copy(i, hop):
        src, dst = weights[i]
        if hop == 2:
            src, block = dst.at[w_rows(across), :], across
        else:
            block = t
        target = across if hop == 0 else sibling
        return pltpu.make_async_remote_copy(
            src_ref=src,
            dst_ref=dst.at[w_rows(block), :],
            send_sem=w_send.at[i, hop],
            recv_sem=w_recv.at[i, hop],
            device_id=(z * TENANTS + target, y),
            device_id_type=MESH,
        )

    mix_copy = pltpu.make_async_remote_copy(
        src_ref=mix_all.at[y],
        dst_ref=mix_all.at[y],
        send_sem=mix_send,
        recv_sem=mix_recv,
        device_id=(place, other),
        device_id_type=MESH,
    )

    for a in range(6):
        own_copy(a).start()
    for i in range(2):
        w_own(i).start()
    mix_own = pltpu.make_async_copy(mix_ref, mix_all.at[y], mix_local)
    mix_own.start()
    frac = 1.0 - jnp.full(sigma_ref.shape, step_ref[t], jnp.int32).astype(jnp.float32) / STEPS
    sigma_ref[...] = 5.0 * frac / (1.0 + 4.0 * frac)
    for ref, filled in ((k_all, rows), (v_all, rows), (tk_all, group * tk_in.shape[0]), (tv_all, group * tv_in.shape[0])):
        if ref.shape[0] > filled:
            ref[filled:, :] = jnp.zeros((ref.shape[0] - filled, ref.shape[1]), ref.dtype)

    pl.semaphore_wait(barrier, len(friends))

    def send_half(h, i):
        for a in range(3 * i, 3 * i + 3):
            for k in range(group - 1, 0, -1):
                in_copy(a, h, k).start()

    ahead = min(2, heads_here)
    send_half(0, 0)
    send_half(0, 1)
    for i in range(2):
        w_copy(i, 0).start()
    for h in range(1, ahead):
        send_half(h, 0)
        send_half(h, 1)
    for i in range(2):
        w_copy(i, 1).start()
    mix_own.wait()
    mix_copy.start()
    for a in range(6):
        own_copy(a).wait()

    gathered = [so_all, co_all]

    window = half * tiles + 16
    spans = [(0, window), (window, rows - window)]
    late = heads_here

    def at_copy(i, h, source, way):
        width = DH
        head, span = h, spans[0]
        if isinstance(h, int) and h == late:
            head, span, width = 0, spans[1], heads_here * DH
        column = pl.ds(pl.multiple_of((source * heads_here + head) * DH, DH), width)
        return pltpu.make_async_remote_copy(
            src_ref=gathered[i].at[pl.ds(*span), column],
            dst_ref=gathered[i].at[pl.ds(*span), column],
            send_sem=at_send.at[i, h, source, way],
            recv_sem=at_recv.at[i, h, source],
            device_id=((z + 1 - 2 * way) * TENANTS + t, y),
            device_id_type=MESH,
        )

    def both_ways(i, h, d, act):
        for way in range(2):
            source = z - d if way == 0 else z + d
            onward = z < group - 1 if way == 0 else z > 0
            here = source >= 0 if way == 0 else source < group

            @pl.when(here)
            def _():
                act(at_copy(i, h, source, way), onward)

    def relay(i, h, d):
        def act(copy, onward):
            if d > 0:
                copy.wait_recv()

            @pl.when(onward)
            def _():
                copy.start()

        both_ways(i, h, d, act)

    def settle(i, h, d):
        def act(copy, onward):
            @pl.when(onward)
            def _():
                copy.wait_send()

        both_ways(i, h, d, act)

    def do_head(h, carry):
        here = pl.ds(pl.multiple_of(h * DH, DH), DH)
        column = pl.ds(pl.multiple_of((z * heads_here + h) * DH, DH), DH)
        for i, (qr, kr, vr, count) in enumerate(
            ((q_all, k_all, v_all, my_len), (cq_all, tk_all, tv_all, my_text))
        ):
            for a in range(3 * i, 3 * i + 3):
                for k in range(1, group):
                    in_copy(a, h, k).wait_recv()

            @pl.when(h == heads_here - 1)
            def _():
                w_copy(i, 0).wait_recv()
                w_copy(i, 2).start()

            @pl.when(h + ahead < heads_here)
            def _():
                send_half(h + ahead, i)

            gathered[i][:, column] = attend_head(qr[:, here], kr[:, here], vr[:, here], count)
            relay(i, h, 0)
            for d in range(1, group):
                back = i - d
                older = h + back // 2

                @pl.when(older >= 0)
                def _():
                    relay(back % 2, older, d)

        return carry

    lax.fori_loop(0, heads_here, do_head, 0)

    side = term.shape[1]
    lead = side % 256
    chunks = [(0, lead)] if lead else []
    chunks += [(at, 256) for at in range(lead, side, 256)]

    def term_copy(part, j):
        at, n = chunks[j]
        where = (pl.ds(*spans[part]), pl.ds(at, n))
        return pltpu.make_async_remote_copy(
            src_ref=term.at[where],
            dst_ref=term_in.at[where],
            send_sem=term_send.at[part, j],
            recv_sem=term_recv.at[part, j],
            device_id=(place, other),
            device_id_type=MESH,
        )

    def project(part, whose, j):
        at, n = chunks[j]
        lo, count = spans[part]
        start = pl.multiple_of(whose * side + at, 128)
        first = pl.multiple_of(z * (2 * side) + whose * side + at, 128)
        gates = gate_ref[:, pl.ds(first, n)]
        mine = lax.broadcasted_iota(jnp.int32, gates.shape, 0) == t
        gates = jnp.sum(jnp.where(mine, gates, 0.0), axis=0, keepdims=True)

        def product(left, right):
            return lax.dot_general(
                left[lo : lo + count, :],
                right[pl.ds(start, n), :],
                (((1,), (1,)), ((), ())),
                preferred_element_type=jnp.float32,
            )

        return (gates * product(so_all, ws_all) + product(co_all, wc_all)).astype(jnp.bfloat16)

    source = lax.rem(z, half) * 2 + y

    def out_columns(sender, j):
        at, n = chunks[j]
        return pl.ds(pl.multiple_of(sender * side + at, 128), n)

    def vel_part(j, to):
        at, n = chunks[j]
        return vel.at[pl.ds(to * tiles, tiles), pl.ds(at, n)]

    def out_copy(j, to):
        return pltpu.make_async_remote_copy(
            src_ref=vel_part(j, to),
            dst_ref=out.at[:, out_columns(source, j)],
            send_sem=out_send.at[j, to],
            recv_sem=out_recv.at[source, j],
            device_id=(to * TENANTS + t, y_out),
            device_id_type=MESH,
        )

    def out_own(j, to):
        return pltpu.make_async_copy(
            vel_part(j, to), out.at[:, out_columns(source, j)], out_local.at[j]
        )

    def stays(to):
        return jnp.logical_and(z == to, y_out == y)

    def send_out(j, to):
        @pl.when(stays(to))
        def _():
            out_own(j, to).start()

        @pl.when(jnp.logical_not(stays(to)))
        def _():
            out_copy(j, to).start()

    def finish_out(j, to):
        @pl.when(stays(to))
        def _():
            out_own(j, to).wait()

        @pl.when(jnp.logical_not(stays(to)))
        def _():
            out_copy(j, to).wait_send()

    def swap(part):
        lo, count = spans[part]
        for j, (at, n) in enumerate(chunks):
            term[lo : lo + count, at : at + n] = project(part, other, j)
            term_copy(part, j).start()

    def keep(part):
        lo, count = spans[part]
        for j, (at, n) in enumerate(chunks):
            term_own[lo : lo + count, at : at + n] = project(part, y, j)

    def smooth(part):
        lo = part * (rows - window)
        skip = part * 16
        for j, (at, n) in enumerate(chunks):
            term_copy(part, j).wait_recv()
            total = term_own[lo : lo + window, at : at + n].astype(jnp.float32)
            total = total + term_in[lo : lo + window, at : at + n].astype(jnp.float32)
            branch = total.astype(jnp.bfloat16).astype(jnp.float32)
            index = lo + lax.broadcasted_iota(jnp.int32, branch.shape, 0)
            branch = jnp.where(index < my_len, branch, 0.0)
            before = jnp.where(index == 0, 0.0, pltpu.roll(branch, 1, 0))
            after = jnp.where(index == rows - 1, 0.0, pltpu.roll(branch, window - 1, 0))
            line = (source * side + at) // DH
            mix = jnp.concatenate(
                [mix_all[y_out, pl.ds(line + m, 1), :] for m in range(n // DH)], axis=1
            )
            speed = branch + mix * (before + after - 2.0 * branch)
            speed = jnp.where(index < my_len, speed, 0.0).astype(jnp.bfloat16)
            vel[lo + skip : lo + skip + half * tiles, at : at + n] = speed[skip : skip + half * tiles]
            for to in range(part * half, part * half + half):
                send_out(j, to)

    pieces = 2 * heads_here
    for i in range(2):
        relay(i, late, 0)
    for step in range(pieces, pieces + group - 1):
        for d in range(1, group):
            if step - d < pieces:
                relay((step - d) % 2, (step - d) // 2, d)
    for i in range(2):
        w_own(i).wait()
        w_copy(i, 1).wait_recv()
    for i in range(2):
        w_copy(i, 2).wait_recv()
    mix_copy.wait_recv()
    stages = [lambda: swap(0), lambda: keep(0), lambda: smooth(0)]
    for d in range(1, group):
        for i in range(2):
            relay(i, late, d)
        if d < group - 1 and stages:
            stages.pop(0)()
        if d == group - 2:
            while stages:
                stages.pop(0)()
    while stages:
        stages.pop(0)()
    swap(1)
    keep(1)
    smooth(1)

    def drain_head(h, carry):
        for k in range(1, group):
            for a in range(6):
                in_copy(a, h, k).wait_send()
        for i in range(2):
            for d in range(group - 1):
                settle(i, h, d)
        return carry

    lax.fori_loop(0, heads_here, drain_head, 0)
    for i in range(2):
        for hop in range(3):
            w_copy(i, hop).wait_send()
    mix_copy.wait_send()

    for i in range(2):
        for d in range(group - 1):
            settle(i, late, d)
    for j in range(len(chunks)):
        for part in range(2):
            term_copy(part, j).wait_send()
        for to in range(group):
            finish_out(j, to)

    def arrive(sender, carry):
        mine = jnp.logical_and(y_out == y, sender == source)

        @pl.when(jnp.logical_not(mine))
        def _():
            for j in range(len(chunks)):
                pltpu.make_async_remote_copy(
                    src_ref=vel_part(j, 0),
                    dst_ref=out.at[:, out_columns(sender, j)],
                    send_sem=out_send.at[j, 0],
                    recv_sem=out_recv.at[sender, j],
                    device_id=(place, other),
                    device_id_type=MESH,
                ).wait_recv()

        return carry

    lax.fori_loop(0, group, arrive, 0)


def fits(query, text_key, wo_self):
    group = lax.axis_size("req") // TENANTS
    heads = query.shape[1] // DH
    return (
        lax.axis_size("tp") == 2
        and group >= 2
        and group % 2 == 0
        and heads % group == 0
        and query.shape[0] % 16 == 0
        and text_key.shape[0] % 16 == 0
        and wo_self.shape[0] == query.shape[1]
        and wo_self.shape[1] % 64 == 0
    )


def by_heads(
    query,
    key,
    value,
    cross_query,
    text_key,
    text_value,
    wo_self,
    wo_cross,
    attn_gate,
    mix_coef,
    latent,
    tenant_len,
    text_len,
    t_index,
):
    tiles, feat = query.shape
    text_rows = text_key.shape[0]
    blocks = lax.axis_size("req")
    group = blocks // TENANTS
    cols = wo_self.shape[1]
    heads_here = feat // DH // group
    width = heads_here * DH
    rows = tiles * group
    padded = -(-rows // 128) * 128
    texts = -(-text_rows * group // 128) * 128
    side = cols * TENANTS // 2
    chunks = -(-side // 256)
    mix = mix_coef.reshape(-1, DH)
    bf = jnp.bfloat16
    dma = pltpu.SemaphoreType.DMA
    any_spec = pl.BlockSpec(memory_space=pltpu.HBM)
    smem = pl.BlockSpec(memory_space=pltpu.SMEM)
    vmem = pl.BlockSpec(memory_space=pltpu.VMEM)
    flops = 4 * rows * width * (padded + texts) + 4 * rows * feat * TENANTS * cols
    velocity, sigma = pl.pallas_call(
        functools.partial(fused_kernel, group),
        out_shape=(
            jax.ShapeDtypeStruct((tiles, blocks // 2 * cols), bf),
            jax.ShapeDtypeStruct((1, 128), jnp.float32),
        ),
        in_specs=[smem] * 3 + [any_spec] * 8 + [vmem, any_spec],
        out_specs=(any_spec, vmem),
        scratch_shapes=[
            pltpu.VMEM((rows, width), bf),
            pltpu.VMEM((padded, width), bf),
            pltpu.VMEM((padded, width), bf),
            pltpu.VMEM((rows, width), bf),
            pltpu.VMEM((texts, width), bf),
            pltpu.VMEM((texts, width), bf),
            pltpu.VMEM((rows, feat), bf),
            pltpu.VMEM((rows, feat), bf),
            pltpu.VMEM((TENANTS * cols, feat), bf),
            pltpu.VMEM((TENANTS * cols, feat), bf),
            pltpu.VMEM((2, blocks // 2 * cols // DH, DH), jnp.float32),
            pltpu.VMEM((rows, side), bf),
            pltpu.VMEM((rows, side), bf),
            pltpu.VMEM((rows, side), bf),
            pltpu.VMEM((rows, side), bf),
            dma((6, heads_here, group - 1)),
            dma((6, heads_here, group - 1)),
            dma((6,)),
            dma((2, 3)),
            dma((2, 3)),
            dma((2,)),
            dma,
            dma,
            dma,
            dma((2, heads_here + 1, group, 2)),
            dma((2, heads_here + 1, group)),
            dma((2, chunks)),
            dma((2, chunks)),
            dma((chunks, group)),
            dma((group, chunks)),
            dma((chunks,)),
        ],
        compiler_params=pltpu.CompilerParams(
            collective_id=0, has_side_effects=True, vmem_limit_bytes=60 * 1024 * 1024
        ),
        cost_estimate=pl.CostEstimate(
            flops=flops, bytes_accessed=16 * feat * cols, transcendentals=rows * heads_here * (padded + texts)
        ),
        name="attend_project",
    )(
        tenant_len,
        text_len,
        t_index,
        query,
        key,
        value,
        cross_query,
        text_key,
        text_value,
        wo_self.T,
        wo_cross.T,
        attn_gate,
        mix,
    )
    return (velocity, latent.astype(jnp.float32) + sigma[0, 0] * velocity.astype(jnp.float32))


def either(*arrays):
    if fits(arrays[0], arrays[4], arrays[6]):
        return by_heads(*arrays)
    return shards(*arrays)


def solution(mesh):
    placed = (
        P("req", "tp"),
        P("req", "tp"),
        P("req", "tp"),
        P("req", "tp"),
        P("req", "tp"),
        P("req", "tp"),
        P("tp", "req"),
        P("tp", "req"),
        P(),
        P("tp"),
        P("req", "tp"),
        P(),
        P(),
        P(),
    )
    return jax.shard_map(
        either,
        mesh=mesh,
        in_specs=placed,
        out_specs=(P("req", "tp"), P("req", "tp")),
        check_vma=False,
    )
```

```python
import functools

import jax
import jax.numpy as jnp
from jax import lax
from jax.experimental import pallas as pl
from jax.experimental.pallas import tpu as pltpu
from jax.sharding import PartitionSpec as P

DH = 128
TENANTS = 4
STEPS = 50


def passed_along(block, axis, distance):
    devices = range(lax.axis_size(axis))
    route = [((i - distance) % len(devices), i) for i in devices]
    return lax.ppermute(block, axis, route)


def shifted(block, axis, distance):
    devices = range(lax.axis_size(axis))
    route = [(i - distance, i) for i in devices if i - distance in devices]
    return lax.ppermute(block, axis, route)


def attend_block(state, q_heads, k_block, v_block, valid):
    top, denom, accum = state
    heads = q_heads.shape[1]
    k_heads = k_block.reshape(k_block.shape[0], heads, DH)
    v_heads = v_block.reshape(v_block.shape[0], heads, DH)
    scores = jnp.einsum("qhd,khd->hqk", q_heads, k_heads, preferred_element_type=jnp.float32) * (
        1.0 / DH**0.5
    )
    scores = jnp.where(valid[None, None, :], scores, -1e30)
    new_top = jnp.maximum(top, jnp.max(scores, axis=-1))
    weights = jnp.where(valid[None, None, :], jnp.exp(scores - new_top[..., None]), 0.0)
    factor = jnp.exp(top - new_top)
    denom = denom * factor + jnp.sum(weights, axis=-1)
    mixed = jnp.einsum(
        "hqk,khd->hqd", weights.astype(jnp.bfloat16), v_heads, preferred_element_type=jnp.float32
    )
    return (new_top, denom, accum * factor[..., None] + mixed)


def finish(state, tiles, feat):
    top, denom, accum = state
    out = accum / denom[..., None]
    return out.transpose(1, 0, 2).reshape(tiles, feat).astype(jnp.bfloat16)


def shards(
    query,
    key,
    value,
    cross_query,
    text_key,
    text_value,
    wo_self,
    wo_cross,
    attn_gate,
    mix_coef,
    latent,
    tenant_len,
    text_len,
    t_index,
):
    tiles, feat = query.shape
    text_rows = text_key.shape[0]
    heads = feat // DH
    group = lax.axis_size("req") // TENANTS
    place = lax.axis_index("req")
    tenant = place % TENANTS
    slot = place // TENANTS
    picker = jnp.arange(TENANTS) == tenant
    my_len = jnp.sum(jnp.where(picker, tenant_len, 0))
    my_text = jnp.sum(jnp.where(picker, text_len, 0))
    my_step = jnp.sum(jnp.where(picker, t_index, 0))
    gate_row = jnp.sum(jnp.where(picker[:, None], attn_gate, 0.0), axis=0)
    q_heads = query.reshape(tiles, heads, DH)
    cq_heads = cross_query.reshape(tiles, heads, DH)
    row_ids = jnp.arange(tiles, dtype=jnp.int32)

    def absorb(held, blocks, root):
        state, text_keys, text_values = held
        k_block, v_block, tk_block, tv_block = blocks
        valid = root * tiles + row_ids < my_len
        state = attend_block(state, q_heads, k_block, v_block, valid)
        text_keys = lax.dynamic_update_slice_in_dim(text_keys, tk_block, root * text_rows, 0)
        text_values = lax.dynamic_update_slice_in_dim(text_values, tv_block, root * text_rows, 0)
        return (state, text_keys, text_values)

    def fresh(count):
        return (
            jnp.full((heads, count), -1e30, jnp.float32),
            jnp.zeros((heads, count), jnp.float32),
            jnp.zeros((heads, count, DH), jnp.float32),
        )

    all_text = group * text_rows
    empty_text = jnp.zeros((all_text, feat), text_key.dtype)
    start_blocks = (key, value, text_key, text_value)
    held = absorb((fresh(tiles), empty_text, empty_text), start_blocks, slot)

    def turn_cycle(j, carry):
        blocks, kept = carry
        blocks = passed_along((blocks[0], blocks[1], blocks[2], blocks[3]), "req", TENANTS)
        return (blocks, absorb(kept, blocks, (slot - j) % group))

    _, held = lax.fori_loop(1, group, turn_cycle, (start_blocks, held))
    self_state, text_keys, text_values = held
    self_out = finish(self_state, tiles, feat)
    text_valid = jnp.arange(all_text, dtype=jnp.int32) < my_text
    cross_state = attend_block(fresh(tiles), cq_heads, text_keys, text_values, text_valid)
    cross_out = finish(cross_state, tiles, feat)
    self_cols = lax.all_gather(wo_self, "req", axis=1, tiled=True)
    cross_cols = lax.all_gather(wo_cross, "req", axis=1, tiled=True)
    block = gate_row[None, :] * jnp.dot(self_out, self_cols, preferred_element_type=jnp.float32)
    block = block + jnp.dot(cross_out, cross_cols, preferred_element_type=jnp.float32)
    summed = lax.psum_scatter(block.astype(jnp.bfloat16), "tp", scatter_dimension=1, tiled=True)
    valid_rows = slot * tiles + row_ids < my_len
    branch = jnp.where(valid_rows[:, None], summed, jnp.zeros((), jnp.bfloat16))
    before = shifted(branch[-1:], "req", TENANTS)
    after = shifted(branch[:1], "req", -TENANTS)
    extended = jnp.concatenate([before, branch, after], axis=0).astype(jnp.float32)
    branch32 = branch.astype(jnp.float32)
    vel = branch32 + mix_coef[None, :] * (extended[:-2] + extended[2:] - 2.0 * branch32)
    vel = jnp.where(valid_rows[:, None], vel, 0.0)
    frac = 1.0 - my_step.astype(jnp.float32) / STEPS
    sigma = 5.0 * frac / (1.0 + 4.0 * frac)
    updated = latent.astype(jnp.float32) + sigma * vel
    return (vel.astype(jnp.bfloat16), updated)


MESH = pl.DeviceIdType.MESH


def attend_head(q, k, v, count):
    scores = lax.dot_general(
        q, k, (((1,), (1,)), ((), ())), preferred_element_type=jnp.float32
    ) * (1.0 / DH**0.5)
    valid = lax.broadcasted_iota(jnp.int32, scores.shape, 1) < count
    scores = jnp.where(valid, scores, -1e30)
    top = jnp.max(scores, axis=-1, keepdims=True)
    weights = jnp.where(valid, jnp.exp(scores - top), 0.0)
    denom = jnp.sum(weights, axis=-1, keepdims=True)
    mixed = jnp.dot(weights.astype(jnp.bfloat16), v, preferred_element_type=jnp.float32)
    return (mixed / denom).astype(jnp.bfloat16)


def fused_kernel(
    group,
    len_ref,
    text_ref,
    step_ref,
    q_in,
    k_in,
    v_in,
    cq_in,
    tk_in,
    tv_in,
    ws_in,
    wc_in,
    gate_ref,
    mix_ref,
    out,
    sigma_ref,
    q_all,
    k_all,
    v_all,
    cq_all,
    tk_all,
    tv_all,
    so_all,
    co_all,
    ws_all,
    wc_all,
    mix_all,
    term,
    term_own,
    term_in,
    vel,
    in_send,
    in_recv,
    in_local,
    w_send,
    w_recv,
    w_local,
    mix_local,
    mix_send,
    mix_recv,
    at_send,
    at_recv,
    term_send,
    term_recv,
    out_send,
    out_recv,
    out_local,
):
    place = lax.axis_index("req")
    y = lax.axis_index("tp")
    t = lax.rem(place, TENANTS)
    z = place // TENANTS
    half = group // 2
    tiles = q_in.shape[0]
    rows = tiles * group
    heads_here = q_in.shape[1] // (DH * group)
    sibling = t + 1 - 2 * lax.rem(t, 2)
    across = lax.rem(t + 2, TENANTS)
    other = 1 - y
    y_out = z // half
    my_len = len_ref[t]
    my_text = text_ref[t]

    def peer(k):
        return lax.rem(z + k, group)

    barrier = pltpu.get_barrier_semaphore()
    friends = [(z * TENANTS + sibling, y), (z * TENANTS + across, y), (place, other)]
    for k in range(1, group):
        friends += [(peer(k) * TENANTS + t, y), (peer(k) * TENANTS + t, other)]
    for friend in friends:
        pl.semaphore_signal(barrier, inc=1, device_id=friend, device_id_type=MESH)

    moved = [
        (q_in, q_all),
        (k_in, k_all),
        (v_in, v_all),
        (cq_in, cq_all),
        (tk_in, tk_all),
        (tv_in, tv_all),
    ]

    def own_copy(a):
        src, dst = moved[a]
        n = src.shape[0]
        width = heads_here * DH
        return pltpu.make_async_copy(
            src.at[:, pl.ds(pl.multiple_of(z * width, DH), width)],
            dst.at[pl.ds(pl.multiple_of(z * n, 16), n), :],
            in_local.at[a],
        )

    def in_copy(a, h, k):
        src, dst = moved[a]
        n = src.shape[0]
        to = peer(k)
        return pltpu.make_async_remote_copy(
            src_ref=src.at[:, pl.ds(pl.multiple_of((to * heads_here + h) * DH, DH), DH)],
            dst_ref=dst.at[
                pl.ds(pl.multiple_of(z * n, 16), n), pl.ds(pl.multiple_of(h * DH, DH), DH)
            ],
            send_sem=in_send.at[a, h, k - 1],
            recv_sem=in_recv.at[a, h, k - 1],
            device_id=(to * TENANTS + t, y),
            device_id_type=MESH,
        )

    weights = [(ws_in, ws_all), (wc_in, wc_all)]

    cols = ws_in.shape[0]

    def w_rows(block):
        return pl.ds(pl.multiple_of(block * cols, 16), cols)

    def w_own(i):
        src, dst = weights[i]
        return pltpu.make_async_copy(src, dst.at[w_rows(t), :], w_local.at[i])

    bounds = [cols // 16 * c // heads_here * 16 for c in range(heads_here + 1)]

    def w_copy(i, hop, c):
        src, dst = weights[i]
        low, n = bounds[c], bounds[c + 1] - bounds[c]
        block = across if hop == 2 else t
        there = dst.at[pl.ds(pl.multiple_of(block * cols + low, 16), n), :]
        target = across if hop == 0 else sibling
        return pltpu.make_async_remote_copy(
            src_ref=there if hop == 2 else src.at[pl.ds(low, n), :],
            dst_ref=there,
            send_sem=w_send.at[i, hop, c],
            recv_sem=w_recv.at[i, hop, c],
            device_id=(z * TENANTS + target, y),
            device_id_type=MESH,
        )

    mix_copy = pltpu.make_async_remote_copy(
        src_ref=mix_all.at[y],
        dst_ref=mix_all.at[y],
        send_sem=mix_send,
        recv_sem=mix_recv,
        device_id=(place, other),
        device_id_type=MESH,
    )

    for a in range(6):
        own_copy(a).start()
    for i in range(2):
        w_own(i).start()
    mix_own = pltpu.make_async_copy(mix_ref, mix_all.at[y], mix_local)
    mix_own.start()
    frac = 1.0 - jnp.full(sigma_ref.shape, step_ref[t], jnp.int32).astype(jnp.float32) / STEPS
    sigma_ref[...] = 5.0 * frac / (1.0 + 4.0 * frac)
    for ref, filled in ((k_all, rows), (v_all, rows), (tk_all, group * tk_in.shape[0]), (tv_all, group * tv_in.shape[0])):
        if ref.shape[0] > filled:
            ref[filled:, :] = jnp.zeros((ref.shape[0] - filled, ref.shape[1]), ref.dtype)

    pl.semaphore_wait(barrier, len(friends))

    def send_half(h, i):
        for a in range(3 * i, 3 * i + 3):
            for k in range(group - 1, 0, -1):
                in_copy(a, h, k).start()

    ahead = min(2, heads_here)
    send_half(0, 0)
    send_half(0, 1)
    for i in range(2):
        w_copy(i, 0, 0).start()
    for h in range(1, ahead):
        send_half(h, 0)
        send_half(h, 1)
    mix_own.wait()
    mix_copy.start()
    for a in range(6):
        own_copy(a).wait()

    gathered = [so_all, co_all]

    window = half * tiles + 16
    spans = [(0, window), (window, rows - window)]
    late = heads_here

    def at_copy(i, h, source, way):
        width = DH
        head, span = h, spans[0]
        if isinstance(h, int) and h == late:
            head, span, width = 0, spans[1], heads_here * DH
        column = pl.ds(pl.multiple_of((source * heads_here + head) * DH, DH), width)
        return pltpu.make_async_remote_copy(
            src_ref=gathered[i].at[pl.ds(*span), column],
            dst_ref=gathered[i].at[pl.ds(*span), column],
            send_sem=at_send.at[i, h, source, way],
            recv_sem=at_recv.at[i, h, source],
            device_id=((z + 1 - 2 * way) * TENANTS + t, y),
            device_id_type=MESH,
        )

    def both_ways(i, h, d, act):
        for way in range(2):
            source = z - d if way == 0 else z + d
            onward = z < group - 1 if way == 0 else z > 0
            here = source >= 0 if way == 0 else source < group

            @pl.when(here)
            def _():
                act(at_copy(i, h, source, way), onward)

    def relay(i, h, d):
        def act(copy, onward):
            if d > 0:
                copy.wait_recv()

            @pl.when(onward)
            def _():
                copy.start()

        both_ways(i, h, d, act)

    def settle(i, h, d):
        def act(copy, onward):
            @pl.when(onward)
            def _():
                copy.wait_send()

        both_ways(i, h, d, act)

    def do_head(h, carry):
        here = pl.ds(pl.multiple_of(h * DH, DH), DH)
        column = pl.ds(pl.multiple_of((z * heads_here + h) * DH, DH), DH)
        for i, (qr, kr, vr, count) in enumerate(
            ((q_all, k_all, v_all, my_len), (cq_all, tk_all, tv_all, my_text))
        ):
            for a in range(3 * i, 3 * i + 3):
                for k in range(1, group):
                    in_copy(a, h, k).wait_recv()

            @pl.when(h + ahead < heads_here)
            def _():
                send_half(h + ahead, i)

            gathered[i][:, column] = attend_head(qr[:, here], kr[:, here], vr[:, here], count)
            relay(i, h, 0)
            for c in range(heads_here):

                @pl.when(h == c)
                def _():
                    if c + 1 < heads_here:
                        w_copy(i, 0, c + 1).start()
                    w_copy(i, 1, c).start()
                    if c > 0:
                        w_copy(i, 0, c - 1).wait_recv()
                        w_copy(i, 2, c - 1).start()

            for d in range(1, group):
                back = i - d
                older = h + back // 2

                @pl.when(older >= 0)
                def _():
                    relay(back % 2, older, d)

        return carry

    lax.fori_loop(0, heads_here, do_head, 0)

    side = term.shape[1]
    lead = side % 256
    chunks = [(0, lead)] if lead else []
    chunks += [(at, 256) for at in range(lead, side, 256)]

    def term_copy(part, j):
        at, n = chunks[j]
        where = (pl.ds(*spans[part]), pl.ds(at, n))
        return pltpu.make_async_remote_copy(
            src_ref=term.at[where],
            dst_ref=term_in.at[where],
            send_sem=term_send.at[part, j],
            recv_sem=term_recv.at[part, j],
            device_id=(place, other),
            device_id_type=MESH,
        )

    def project(part, whose, j):
        at, n = chunks[j]
        lo, count = spans[part]
        start = pl.multiple_of(whose * side + at, 128)
        first = pl.multiple_of(z * (2 * side) + whose * side + at, 128)
        gates = gate_ref[:, pl.ds(first, n)]
        mine = lax.broadcasted_iota(jnp.int32, gates.shape, 0) == t
        gates = jnp.sum(jnp.where(mine, gates, 0.0), axis=0, keepdims=True)

        def product(left, right):
            return lax.dot_general(
                left[lo : lo + count, :],
                right[pl.ds(start, n), :],
                (((1,), (1,)), ((), ())),
                preferred_element_type=jnp.float32,
            )

        return (gates * product(so_all, ws_all) + product(co_all, wc_all)).astype(jnp.bfloat16)

    source = lax.rem(z, half) * 2 + y

    def out_columns(sender, j):
        at, n = chunks[j]
        return pl.ds(pl.multiple_of(sender * side + at, 128), n)

    def vel_part(j, to):
        at, n = chunks[j]
        return vel.at[pl.ds(to * tiles, tiles), pl.ds(at, n)]

    def out_copy(j, to):
        return pltpu.make_async_remote_copy(
            src_ref=vel_part(j, to),
            dst_ref=out.at[:, out_columns(source, j)],
            send_sem=out_send.at[j, to],
            recv_sem=out_recv.at[source, j],
            device_id=(to * TENANTS + t, y_out),
            device_id_type=MESH,
        )

    def out_own(j, to):
        return pltpu.make_async_copy(
            vel_part(j, to), out.at[:, out_columns(source, j)], out_local.at[j]
        )

    def stays(to):
        return jnp.logical_and(z == to, y_out == y)

    def send_out(j, to):
        @pl.when(stays(to))
        def _():
            out_own(j, to).start()

        @pl.when(jnp.logical_not(stays(to)))
        def _():
            out_copy(j, to).start()

    def finish_out(j, to):
        @pl.when(stays(to))
        def _():
            out_own(j, to).wait()

        @pl.when(jnp.logical_not(stays(to)))
        def _():
            out_copy(j, to).wait_send()

    def swap(part):
        lo, count = spans[part]
        for j, (at, n) in enumerate(chunks):
            term[lo : lo + count, at : at + n] = project(part, other, j)
            term_copy(part, j).start()

    def keep(part):
        lo, count = spans[part]
        for j, (at, n) in enumerate(chunks):
            term_own[lo : lo + count, at : at + n] = project(part, y, j)

    def smooth(part):
        lo = part * (rows - window)
        skip = part * 16
        for j, (at, n) in enumerate(chunks):
            term_copy(part, j).wait_recv()
            total = term_own[lo : lo + window, at : at + n].astype(jnp.float32)
            total = total + term_in[lo : lo + window, at : at + n].astype(jnp.float32)
            branch = total.astype(jnp.bfloat16).astype(jnp.float32)
            index = lo + lax.broadcasted_iota(jnp.int32, branch.shape, 0)
            branch = jnp.where(index < my_len, branch, 0.0)
            before = jnp.where(index == 0, 0.0, pltpu.roll(branch, 1, 0))
            after = jnp.where(index == rows - 1, 0.0, pltpu.roll(branch, window - 1, 0))
            line = (source * side + at) // DH
            mix = jnp.concatenate(
                [mix_all[y_out, pl.ds(line + m, 1), :] for m in range(n // DH)], axis=1
            )
            speed = branch + mix * (before + after - 2.0 * branch)
            speed = jnp.where(index < my_len, speed, 0.0).astype(jnp.bfloat16)
            vel[lo + skip : lo + skip + half * tiles, at : at + n] = speed[skip : skip + half * tiles]
            for to in range(part * half, part * half + half):
                send_out(j, to)

    pieces = 2 * heads_here
    for i in range(2):
        relay(i, late, 0)
    for i in range(2):
        w_copy(i, 0, heads_here - 1).wait_recv()
        w_copy(i, 2, heads_here - 1).start()
    for step in range(pieces, pieces + group - 1):
        for d in range(1, group):
            if step - d < pieces:
                relay((step - d) % 2, (step - d) // 2, d)
    for i in range(2):
        w_own(i).wait()
        for hop in (1, 2):
            for c in range(heads_here):
                w_copy(i, hop, c).wait_recv()
    mix_copy.wait_recv()
    stages = [lambda: swap(0), lambda: keep(0), lambda: smooth(0)]
    for d in range(1, group):
        for i in range(2):
            relay(i, late, d)
        if d < group - 1 and stages:
            stages.pop(0)()
        if d == group - 2:
            while stages:
                stages.pop(0)()
    while stages:
        stages.pop(0)()
    swap(1)
    keep(1)
    smooth(1)

    def drain_head(h, carry):
        for k in range(1, group):
            for a in range(6):
                in_copy(a, h, k).wait_send()
        for i in range(2):
            for d in range(group - 1):
                settle(i, h, d)
        return carry

    lax.fori_loop(0, heads_here, drain_head, 0)
    for i in range(2):
        for hop in range(3):
            for c in range(heads_here):
                w_copy(i, hop, c).wait_send()
    mix_copy.wait_send()

    for i in range(2):
        for d in range(group - 1):
            settle(i, late, d)
    for j in range(len(chunks)):
        for part in range(2):
            term_copy(part, j).wait_send()
        for to in range(group):
            finish_out(j, to)

    def arrive(sender, carry):
        mine = jnp.logical_and(y_out == y, sender == source)

        @pl.when(jnp.logical_not(mine))
        def _():
            for j in range(len(chunks)):
                pltpu.make_async_remote_copy(
                    src_ref=vel_part(j, 0),
                    dst_ref=out.at[:, out_columns(sender, j)],
                    send_sem=out_send.at[j, 0],
                    recv_sem=out_recv.at[sender, j],
                    device_id=(place, other),
                    device_id_type=MESH,
                ).wait_recv()

        return carry

    lax.fori_loop(0, group, arrive, 0)


def fits(query, text_key, wo_self):
    group = lax.axis_size("req") // TENANTS
    heads = query.shape[1] // DH
    return (
        lax.axis_size("tp") == 2
        and group >= 2
        and group % 2 == 0
        and heads % group == 0
        and query.shape[0] % 16 == 0
        and text_key.shape[0] % 16 == 0
        and wo_self.shape[0] == query.shape[1]
        and wo_self.shape[1] % 64 == 0
    )


def by_heads(
    query,
    key,
    value,
    cross_query,
    text_key,
    text_value,
    wo_self,
    wo_cross,
    attn_gate,
    mix_coef,
    latent,
    tenant_len,
    text_len,
    t_index,
):
    tiles, feat = query.shape
    text_rows = text_key.shape[0]
    blocks = lax.axis_size("req")
    group = blocks // TENANTS
    cols = wo_self.shape[1]
    heads_here = feat // DH // group
    width = heads_here * DH
    rows = tiles * group
    padded = -(-rows // 128) * 128
    texts = -(-text_rows * group // 128) * 128
    side = cols * TENANTS // 2
    chunks = -(-side // 256)
    mix = mix_coef.reshape(-1, DH)
    bf = jnp.bfloat16
    dma = pltpu.SemaphoreType.DMA
    any_spec = pl.BlockSpec(memory_space=pltpu.HBM)
    smem = pl.BlockSpec(memory_space=pltpu.SMEM)
    vmem = pl.BlockSpec(memory_space=pltpu.VMEM)
    flops = 4 * rows * width * (padded + texts) + 4 * rows * feat * TENANTS * cols
    velocity, sigma = pl.pallas_call(
        functools.partial(fused_kernel, group),
        out_shape=(
            jax.ShapeDtypeStruct((tiles, blocks // 2 * cols), bf),
            jax.ShapeDtypeStruct((1, 128), jnp.float32),
        ),
        in_specs=[smem] * 3 + [any_spec] * 8 + [vmem, any_spec],
        out_specs=(any_spec, vmem),
        scratch_shapes=[
            pltpu.VMEM((rows, width), bf),
            pltpu.VMEM((padded, width), bf),
            pltpu.VMEM((padded, width), bf),
            pltpu.VMEM((rows, width), bf),
            pltpu.VMEM((texts, width), bf),
            pltpu.VMEM((texts, width), bf),
            pltpu.VMEM((rows, feat), bf),
            pltpu.VMEM((rows, feat), bf),
            pltpu.VMEM((TENANTS * cols, feat), bf),
            pltpu.VMEM((TENANTS * cols, feat), bf),
            pltpu.VMEM((2, blocks // 2 * cols // DH, DH), jnp.float32),
            pltpu.VMEM((rows, side), bf),
            pltpu.VMEM((rows, side), bf),
            pltpu.VMEM((rows, side), bf),
            pltpu.VMEM((rows, side), bf),
            dma((6, heads_here, group - 1)),
            dma((6, heads_here, group - 1)),
            dma((6,)),
            dma((2, 3, heads_here)),
            dma((2, 3, heads_here)),
            dma((2,)),
            dma,
            dma,
            dma,
            dma((2, heads_here + 1, group, 2)),
            dma((2, heads_here + 1, group)),
            dma((2, chunks)),
            dma((2, chunks)),
            dma((chunks, group)),
            dma((group, chunks)),
            dma((chunks,)),
        ],
        compiler_params=pltpu.CompilerParams(
            collective_id=0, has_side_effects=True, vmem_limit_bytes=60 * 1024 * 1024
        ),
        cost_estimate=pl.CostEstimate(
            flops=flops, bytes_accessed=16 * feat * cols, transcendentals=rows * heads_here * (padded + texts)
        ),
        name="attend_project",
    )(
        tenant_len,
        text_len,
        t_index,
        query,
        key,
        value,
        cross_query,
        text_key,
        text_value,
        wo_self.T,
        wo_cross.T,
        attn_gate,
        mix,
    )
    return (velocity, latent.astype(jnp.float32) + sigma[0, 0] * velocity.astype(jnp.float32))


def either(*arrays):
    if fits(arrays[0], arrays[4], arrays[6]):
        return by_heads(*arrays)
    return shards(*arrays)


def solution(mesh):
    placed = (
        P("req", "tp"),
        P("req", "tp"),
        P("req", "tp"),
        P("req", "tp"),
        P("req", "tp"),
        P("req", "tp"),
        P("tp", "req"),
        P("tp", "req"),
        P(),
        P("tp"),
        P("req", "tp"),
        P(),
        P(),
        P(),
    )
    return jax.shard_map(
        either,
        mesh=mesh,
        in_specs=placed,
        out_specs=(P("req", "tp"), P("req", "tp")),
        check_vma=False,
    )
```
